32 devices in a mesh: queue: 8 (over z, core), head: 4 (over y, x).
Axes of the slice: x: 2, y: 2, z: 4, core: 2. Of those that a mesh axis runs over, the one named last changes fastest.
Arguments:
- latent: bfloat16 [1024, 5120], P(('queue', 'head')), may hold values from -6 to 6
- fresh: bfloat16 [128, 5120], P('head'), may hold values from -6 to 6
- levels: int32 [8], replicated, may hold values from 0 to 47, as said below
- windows: int32 [8], replicated, may hold values from 1 to 8, as said below
- plan: int32 [48], replicated, may hold values from 20 to 975, as said below
- mod_table: float32 [3, 5120], replicated, may hold values from -3 to 3
- w_query: bfloat16 [5120, 4096], P(None, 'head'), may hold values from -0.078125 to 0.078125
- w_key: bfloat16 [5120, 4096], P(None, 'head'), may hold values from -0.078125 to 0.078125
- w_value: bfloat16 [5120, 4096], P(None, 'head'), may hold values from -0.078125 to 0.078125
- w_out: bfloat16 [4096, 5120], P('head'), may hold values from -0.09375 to 0.09375
- query_gain: float32 [4096], P('head'), may hold values from 0.7 to 4, as said below
- key_gain: float32 [4096], P('head'), may hold values from 0.7 to 4, as said below
Outputs:
- velocity: bfloat16 [2, 1024, 5120], P(None, ('queue', 'head'))
- updated: bfloat16 [1024, 5120], P(('queue', 'head'))
The draws below stay inside these ranges and needn't reach their ends.
Inputs may be any that keep to these rules, and one draw needn't show every extreme that they name: `levels`: strictly rising from slot to slot; the first slot has level 0 and the last level 47. `windows`: some slot has window 8 and some slot window 1. `plan`: strictly rising. `query_gain`: positive. `key_gain`: positive.
All inputs are finite; a program needn't handle non-finite values.
Results may differ from the reference program's by a relative error of at most 0.035.
Values may be sent and summed in bfloat16 or wider, within the bound.
A program may use at most 128 MiB of HBM per device.

```python
import math
import jax
import jax.numpy as jnp
from jax import lax

D = 5120
HEADS = 32
HD = 128
LEVELS = 48
STEPS = 2
SLOTS = 8
SPAN = 128
TOKENS = 1024
N_HEAD = 4


def draw_levels(key, part):
    key = jax.random.fold_in(key, 11)
    inner = jax.random.permutation(key, LEVELS - 2)[:SLOTS - 2] + 1
    whole = jnp.concatenate([jnp.zeros((1,), jnp.int32), inner.astype(jnp.int32), jnp.full((1,), LEVELS - 1, jnp.int32)])
    return jnp.sort(whole).astype(jnp.int32)


def draw_windows(key, part):
    key = jax.random.fold_in(key, 12)
    first_key, second_key, third_key = jax.random.split(key, 3)
    base = jax.random.randint(first_key, (SLOTS,), 1, SLOTS + 1)
    widest = jax.random.randint(second_key, (), 0, SLOTS)
    narrow = (widest + 1 + jax.random.randint(third_key, (), 0, SLOTS - 1)) % SLOTS
    base = base.at[widest].set(SLOTS).at[narrow].set(1)
    return base.astype(jnp.int32)


def draw_plan(key, part):
    key = jax.random.fold_in(key, 13)
    jitter = jax.random.randint(key, (LEVELS,), 0, 16)
    jitter = jitter.at[0].set(0).at[LEVELS - 1].set(15)
    return (20 * (jnp.arange(LEVELS) + 1) + jitter).astype(jnp.int32)


def gain_values(key, lower, upper):
    return jnp.exp(jax.random.uniform(key, (HEADS * HD,), jnp.float32, math.log(lower), math.log(upper)))


def draw_query_gain(key, part):
    key = jax.random.fold_in(key, 14)
    return gain_values(key, 0.7, 4.0)


def draw_key_gain(key, part):
    key = jax.random.fold_in(key, 15)
    return gain_values(key, 0.7, 4.0)


def shard_levels(key, shape, shards, smallest, high):
    gain, own = 1.0, jax.random.fold_in(key, 6)
    for axis_at, blocks in shards:
        steps = jnp.exp(jax.random.uniform(jax.random.fold_in(own, axis_at), (blocks,), jnp.float32, smallest / len(shards), high / len(shards)))
        gain = gain * jnp.repeat(steps, shape[axis_at] // blocks).reshape([-1 if axis == axis_at else 1 for axis in range(len(shape))])
    return gain


def centred(rng, shape, scale, bound, cuts=(), held_as=jnp.bfloat16):
    entries = scale * jax.random.normal(rng, shape, jnp.float32)
    if cuts:
        entries = entries * shard_levels(rng, shape, cuts, -0.22, 0.18)
    return jnp.clip(entries, -bound, bound).astype(held_as)


def setup_inputs(seed: int = 0) -> dict:
    streams_of = jax.random.split(jax.random.key(seed), 13)
    latent = centred(streams_of[0], (TOKENS, D), 1.0, 6.0, ((0, 32),))
    fresh = centred(streams_of[1], (SPAN, D), 1.0, 6.0, ((0, 4),))
    levels = draw_levels(jax.random.fold_in(streams_of[12], 71), 0)
    windows = draw_windows(jax.random.fold_in(streams_of[12], 71), 0)
    plan = draw_plan(jax.random.fold_in(streams_of[12], 71), 0)
    mod_table = centred(streams_of[5], (3, D), 0.5, 3.0, (), jnp.float32)
    w_query = centred(streams_of[6], (D, HEADS * HD), D ** -0.5, 0.078125, ((1, 4),))
    w_key = centred(streams_of[7], (D, HEADS * HD), D ** -0.5, 0.078125, ((1, 4),))
    w_value = centred(streams_of[8], (D, HEADS * HD), D ** -0.5, 0.078125, ((1, 4),))
    w_out = centred(streams_of[9], (HEADS * HD, D), (HEADS * HD) ** -0.5, 0.09375, ((0, 4),))
    query_gain = draw_query_gain(jax.random.fold_in(streams_of[12], 71), 0)
    key_gain = draw_key_gain(jax.random.fold_in(streams_of[12], 71), 0)
    return dict(latent=latent, fresh=fresh, levels=levels, windows=windows, plan=plan, mod_table=mod_table, w_query=w_query, w_key=w_key, w_value=w_value, w_out=w_out, query_gain=query_gain, key_gain=key_gain)


def embed(times, width):
    half = width // 2
    freq = jnp.exp(-math.log(10000.0) * jnp.arange(half, dtype=jnp.float32) / half)
    angle = times[:, None] * freq[None, :]
    return jnp.concatenate([jnp.cos(angle), jnp.sin(angle)], axis=-1)

def forward(state, levels, windows, plan, mod_table, w_query, w_key, w_value, w_out, query_gain, key_gain, t_from):
    emb = embed(t_from, D)
    shift = mod_table[0][None, :] + emb
    scale = mod_table[1][None, :] + emb
    gate = mod_table[2][None, :] + emb
    x = state.astype(jnp.float32).reshape(SLOTS, SPAN, D)
    mean = lax.optimization_barrier(jnp.mean(x, axis=-1, keepdims=True))
    var = lax.optimization_barrier(jnp.mean((x - mean) ** 2, axis=-1, keepdims=True))
    h = ((x - mean) * lax.rsqrt(var + 1e-06) * (1.0 + scale[:, None, :]) + shift[:, None, :]).astype(jnp.bfloat16)
    flat = h.reshape(TOKENS, D)
    q = jnp.dot(flat, w_query, preferred_element_type=jnp.float32)
    k = jnp.dot(flat, w_key, preferred_element_type=jnp.float32)
    v = jnp.dot(flat, w_value, preferred_element_type=jnp.float32).astype(jnp.bfloat16)
    qn = (q * lax.rsqrt(lax.optimization_barrier(jnp.mean(q * q, axis=-1, keepdims=True)) + 1e-06) * query_gain).astype(jnp.bfloat16)
    kn = (k * lax.rsqrt(lax.optimization_barrier(jnp.mean(k * k, axis=-1, keepdims=True)) + 1e-06) * key_gain).astype(jnp.bfloat16)
    keys_all = kn.reshape(TOKENS, HEADS, HD).astype(jnp.float32)
    vals_all = v.reshape(TOKENS, HEADS, HD).astype(jnp.float32)
    span_ids = jnp.arange(TOKENS, dtype=jnp.int32) // SPAN

    def attend(index):
        lower = jnp.maximum(0, index - windows[index] + 1)
        valid = (span_ids >= lower) & (span_ids <= index)
        queries = lax.dynamic_slice_in_dim(qn, (index * SPAN).astype(jnp.int32), SPAN, 0)
        queries = queries.reshape(SPAN, HEADS, HD).astype(jnp.float32)
        scores = jnp.einsum('qhd,khd->hqk', queries, keys_all) / math.sqrt(HD)
        masked = jnp.where(valid[None, None, :], scores, -1e+30)
        top = lax.optimization_barrier(jnp.max(masked, axis=-1, keepdims=True))
        weights = jnp.where(valid[None, None, :], jnp.exp(scores - top), 0.0)
        total = lax.optimization_barrier(jnp.sum(weights, axis=-1))
        summed = jnp.einsum('hqk,khd->hqd', weights.astype(jnp.bfloat16).astype(jnp.float32), vals_all)
        out = summed / total[:, :, None]
        return jnp.transpose(out, (1, 0, 2)).reshape(SPAN, HEADS * HD).astype(jnp.bfloat16)
    attn = lax.map(attend, jnp.arange(SLOTS, dtype=jnp.int32)).reshape(TOKENS, HEADS * HD)
    group = HEADS * HD // N_HEAD
    o = jnp.zeros((TOKENS, D), jnp.float32)
    for index in range(N_HEAD):
        part = jnp.dot(attn[:, index * group:(index + 1) * group], w_out[index * group:(index + 1) * group], preferred_element_type=jnp.float32)
        o = o + part.astype(jnp.bfloat16).astype(jnp.float32)
    o = o.reshape(SLOTS, SPAN, D)
    return (x + gate[:, None, :] * o).astype(jnp.bfloat16).reshape(TOKENS, D)

def reference(latent, fresh, levels, windows, plan, mod_table, w_query, w_key, w_value, w_out, query_gain, key_gain):
    t_from = plan[levels].astype(jnp.float32)
    t_to = jnp.concatenate([jnp.zeros((1,), jnp.float32), t_from[:-1]])
    step_size = jnp.repeat((t_to - t_from) / 1000.0, SPAN)[:, None]
    state = latent
    speeds = []
    new = latent
    for step in range(STEPS):
        speed = forward(state, levels, windows, plan, mod_table, w_query, w_key, w_value, w_out, query_gain, key_gain, t_from)
        speeds.append(speed)
        new = (state.astype(jnp.float32) + step_size * speed.astype(jnp.float32)).astype(jnp.bfloat16)
        if step < STEPS - 1:
            state = jnp.concatenate([new[SPAN:], fresh], axis=0)
    return (jnp.stack(speeds), new)
```

```python
import functools
import math

import jax
import jax.numpy as jnp
from jax import lax
from jax.experimental import pallas as pl
from jax.experimental.pallas import tpu as pltpu
from jax.sharding import PartitionSpec as P

HD = 128
STEPS = 2
COLS = 1024
TILE = 512
MESH = pl.DeviceIdType.MESH
VMEM = pl.BlockSpec(memory_space=pltpu.VMEM)
SMEM = pl.BlockSpec(memory_space=pltpu.SMEM)
HBM = pl.BlockSpec(memory_space=pl.ANY)


def greet(axis, me, count):
    barrier = pltpu.get_barrier_semaphore()
    for d in range(1, count):
        pl.semaphore_signal(
            barrier, inc=1, device_id={axis: lax.rem(me + d, count)}, device_id_type=MESH
        )
    pl.semaphore_wait(barrier, count - 1)


def project_kernel(
    heads,
    state_ref,
    shift_ref,
    scale_ref,
    gq_ref,
    gk_ref,
    wq_ref,
    wk_ref,
    wv_ref,
    out_ref,
    gathered,
    weights,
    acc,
    sums,
    sums_in,
    w_sem,
    send_sem,
    recv_sem,
    sum_send,
    sum_recv,
):
    me = lax.axis_index("head")
    rows = state_ref.shape[0]
    chunks = gathered.shape[0]
    span = gathered.shape[1]
    features = wq_ref.shape[1]
    sources = (wq_ref, wk_ref, wv_ref)

    def fetch(c, m):
        at = pl.ds(c * COLS, COLS)
        return pltpu.make_async_copy(
            sources[m].at[at, :], weights.at[m, at, :], w_sem.at[c, m]
        )

    for c in range(chunks):
        for m in range(3):
            fetch(c, m).start()
    x = state_ref[...].astype(jnp.float32)
    mean = jnp.mean(x, axis=-1, keepdims=True)
    var = jnp.mean((x - mean) ** 2, axis=-1, keepdims=True)
    inv = lax.rsqrt(var + 1e-06)
    mine = pl.ds(pl.multiple_of(me * rows, rows), rows)
    greet("head", me, heads)

    def push(c, d, owner):
        block = pl.ds(pl.multiple_of(owner * rows, rows), rows)
        return pltpu.make_async_remote_copy(
            src_ref=gathered.at[c, block, :],
            dst_ref=gathered.at[c, block, :],
            send_sem=send_sem.at[d - 1, c],
            recv_sem=recv_sem.at[d - 1, c],
            device_id={"head": lax.rem(me + d, heads)},
            device_id_type=MESH,
        )

    for c in range(chunks):
        at = slice(c * COLS, (c + 1) * COLS)
        part = state_ref[:, at].astype(jnp.float32)
        normed = (part - mean) * inv * scale_ref[:, at] + shift_ref[:, at]
        gathered[c, mine, :] = normed.astype(jnp.bfloat16)
        for d in range(1, heads):
            push(c, d, me).start()

    acc[...] = jnp.zeros_like(acc)
    tiles = features // TILE

    def multiply(c, m):
        def tile(n, carry):
            at = pl.ds(pl.multiple_of(n * TILE, TILE), TILE)
            acc[m, :, at] += jnp.dot(
                gathered[c],
                weights[m, pl.ds(c * COLS, COLS), at],
                preferred_element_type=jnp.float32,
            )
            return carry

        lax.fori_loop(0, tiles, tile, 0)

    def share(d):
        return pltpu.make_async_remote_copy(
            src_ref=sums,
            dst_ref=sums_in.at[d - 1],
            send_sem=sum_send.at[d - 1],
            recv_sem=sum_recv.at[d - 1],
            device_id={"head": lax.rem(me + d, heads)},
            device_id_type=MESH,
        )

    for c in range(chunks):
        for d in range(1, heads):
            push(c, d, lax.rem(me - d + heads, heads)).wait_recv()
        for m in range(3):
            fetch(c, m).wait()
            if m == 2 and c == chunks - 1:
                for which in range(2):
                    value = acc[which]
                    total = jnp.sum(value * value, axis=-1, keepdims=True)
                    wide = jnp.broadcast_to(total, (span, HD))
                    for part in range(span // HD):
                        turned = jnp.transpose(wide[part * HD : (part + 1) * HD])
                        sums[which, :, part * HD : (part + 1) * HD] = turned[:8]
                for d in range(1, heads):
                    share(d).start()
            multiply(c, m)
    for j in range(features // HD):
        out_ref[j, 2] = acc[2, :, j * HD : (j + 1) * HD].astype(jnp.bfloat16)
    for d in range(1, heads):
        share(d).wait_recv()
    for which, gain_ref in ((0, gq_ref), (1, gk_ref)):
        total = sums[which]
        for d in range(1, heads):
            total = total + sums_in[d - 1, which]
        factor = lax.rsqrt(total / (features * heads) + 1e-06)
        pieces = []
        for part in range(span // HD):
            row = factor[:1, part * HD : (part + 1) * HD]
            pieces.append(jnp.transpose(jnp.broadcast_to(row, (HD, HD))))
        column = jnp.concatenate(pieces, axis=0) if len(pieces) > 1 else pieces[0]
        for j in range(features // HD):
            at = slice(j * HD, (j + 1) * HD)
            out_ref[j, which] = (acc[which, :, at] * column * gain_ref[:, at]).astype(
                jnp.bfloat16
            )
    for d in range(1, heads):
        share(d).wait_send()
        for c in range(chunks):
            push(c, d, me).wait_send()


def attend_kernel(
    slots, windows_ref, qkv_ref, out_ref, held, results, local_sem, send_sem, recv_sem, back_send, back_recv
):
    me = lax.axis_index("queue")
    span = qkv_ref.shape[2]

    def rows_of(slot):
        return pl.ds(pl.multiple_of(slot * span, span), span)

    own = pltpu.make_async_copy(qkv_ref.at[me], held.at[:, rows_of(me), :], local_sem.at[0])
    own.start()
    greet("queue", me, slots)

    def push(d):
        peer = lax.rem(me + d, slots)
        return pltpu.make_async_remote_copy(
            src_ref=qkv_ref.at[peer],
            dst_ref=held.at[:, rows_of(me), :],
            send_sem=send_sem.at[peer],
            recv_sem=recv_sem.at[me],
            device_id={"queue": peer},
            device_id_type=MESH,
        )

    def landed(slot):
        return pltpu.make_async_remote_copy(
            src_ref=qkv_ref.at[slot],
            dst_ref=held.at[:, rows_of(slot), :],
            send_sem=send_sem.at[slot],
            recv_sem=recv_sem.at[slot],
            device_id={"queue": slot},
            device_id_type=MESH,
        )

    def columns_of(head):
        return pl.ds(pl.multiple_of(head * HD, HD), HD)

    def give(slot):
        return pltpu.make_async_remote_copy(
            src_ref=results.at[slot],
            dst_ref=out_ref.at[:, columns_of(me)],
            send_sem=back_send.at[slot],
            recv_sem=back_recv.at[me],
            device_id={"queue": slot},
            device_id_type=MESH,
        )

    def given(head):
        return pltpu.make_async_remote_copy(
            src_ref=results.at[head],
            dst_ref=out_ref.at[:, columns_of(head)],
            send_sem=back_send.at[head],
            recv_sem=back_recv.at[head],
            device_id={"queue": head},
            device_id_type=MESH,
        )

    keep = pltpu.make_async_copy(results.at[me], out_ref.at[:, columns_of(me)], local_sem.at[1])
    for d in range(1, slots):
        push(d).start()
    own.wait()
    for slot in range(slots):

        @pl.when(me != slot)
        def _():
            landed(slot).wait_recv()

        count = (slot + 1) * span
        queries = held[0, slot * span : count, :]
        scores = lax.dot_general(
            queries,
            held[1, :count, :],
            (((1,), (1,)), ((), ())),
            preferred_element_type=jnp.float32,
        ) * (1.0 / math.sqrt(HD))
        ids = lax.broadcasted_iota(jnp.int32, (1, count), 1)
        valid = ids >= (slot - windows_ref[slot] + 1) * span
        masked = jnp.where(valid, scores, -1e30)
        top = jnp.max(masked, axis=-1, keepdims=True)
        weights = jnp.exp(masked - top)
        total = jnp.sum(weights, axis=-1, keepdims=True)
        summed = jnp.dot(
            weights.astype(jnp.bfloat16), held[2, :count, :], preferred_element_type=jnp.float32
        )
        results[slot] = (summed / total).astype(jnp.bfloat16)

        @pl.when(me != slot)
        def _():
            give(slot).start()

        @pl.when(me == slot)
        def _():
            keep.start()

    keep.wait()
    for slot in range(slots):

        @pl.when(me != slot)
        def _():
            given(slot).wait_recv()
            give(slot).wait_send()
            landed(slot).wait_send()


def mix_kernel(
    heads, factor_ref, attn_ref, state_ref, gate_ref, w_ref, speed_ref, new_ref, weights, sent, got, w_sem, send_sem, recv_sem
):
    me = lax.axis_index("head")
    rows = state_ref.shape[0]
    chunks = sent.shape[0]

    def fetch(c):
        return pltpu.make_async_copy(
            w_ref.at[:, pl.ds(c * COLS, COLS)], weights.at[c], w_sem.at[c]
        )

    for c in range(chunks):
        fetch(c).start()
    greet("head", me, heads)

    def push(c, d):
        peer = lax.rem(me + d, heads)
        block = pl.ds(pl.multiple_of(peer * rows, rows), rows)
        return pltpu.make_async_remote_copy(
            src_ref=sent.at[c, block, :],
            dst_ref=got.at[c, d - 1],
            send_sem=send_sem.at[d - 1, c],
            recv_sem=recv_sem.at[d - 1, c],
            device_id={"head": peer},
            device_id_type=MESH,
        )

    for c in range(chunks):
        fetch(c).wait()

        def tile(n, carry, c=c):
            at = pl.ds(pl.multiple_of(n * TILE, TILE), TILE)
            sent[c, :, at] = jnp.dot(
                attn_ref[...], weights[c, :, at], preferred_element_type=jnp.float32
            ).astype(jnp.bfloat16)
            return carry

        lax.fori_loop(0, COLS // TILE, tile, 0)
        for d in range(1, heads):
            push(c, d).start()
    mine = pl.ds(pl.multiple_of(me * rows, rows), rows)
    for c in range(chunks):
        total = sent[c, mine, :].astype(jnp.float32)
        for d in range(1, heads):
            push(c, d).wait_recv()
            total = total + got[c, d - 1].astype(jnp.float32)
        at = slice(c * COLS, (c + 1) * COLS)
        x = state_ref[:, at].astype(jnp.float32)
        speed = (x + gate_ref[:, at] * total).astype(jnp.bfloat16)
        speed_ref[:, at] = speed
        new_ref[:, at] = (x + factor_ref[0] * speed.astype(jnp.float32)).astype(jnp.bfloat16)
    for c in range(chunks):
        for d in range(1, heads):
            push(c, d).wait_send()


def project(state, shift, scale, gq, gk, wq, wk, wv, heads):
    rows, width = state.shape
    span, features = rows * heads, wq.shape[1]
    chunks = width // COLS
    return pl.pallas_call(
        functools.partial(project_kernel, heads),
        out_shape=jax.ShapeDtypeStruct((features // HD, 3, span, HD), jnp.bfloat16),
        in_specs=[VMEM] * 5 + [HBM] * 3,
        out_specs=VMEM,
        scratch_shapes=[
            pltpu.VMEM((chunks, span, COLS), jnp.bfloat16),
            pltpu.VMEM((3, width, features), jnp.bfloat16),
            pltpu.VMEM((3, span, features), jnp.float32),
            pltpu.VMEM((2, 8, span), jnp.float32),
            pltpu.VMEM((heads - 1, 2, 8, span), jnp.float32),
            pltpu.SemaphoreType.DMA((chunks, 3)),
            pltpu.SemaphoreType.DMA((heads - 1, chunks)),
            pltpu.SemaphoreType.DMA((heads - 1, chunks)),
            pltpu.SemaphoreType.DMA((heads - 1,)),
            pltpu.SemaphoreType.DMA((heads - 1,)),
        ],
        compiler_params=pltpu.CompilerParams(
            collective_id=0, has_side_effects=True, vmem_limit_bytes=52 * 2**20
        ),
        cost_estimate=pl.CostEstimate(
            flops=6 * span * width * features, bytes_accessed=6 * width * features, transcendentals=0
        ),
        name="project",
    )(state, shift, scale, gq, gk, wq, wk, wv)


def attend(windows, qkv, slots):
    features, span = qkv.shape[0] * HD, qkv.shape[2]
    return pl.pallas_call(
        functools.partial(attend_kernel, slots),
        out_shape=jax.ShapeDtypeStruct((span, features), jnp.bfloat16),
        in_specs=[SMEM, VMEM],
        out_specs=VMEM,
        scratch_shapes=[
            pltpu.VMEM((3, slots * span, HD), jnp.bfloat16),
            pltpu.VMEM((slots, span, HD), jnp.bfloat16),
            pltpu.SemaphoreType.DMA((2,)),
            pltpu.SemaphoreType.DMA((slots,)),
            pltpu.SemaphoreType.DMA((slots,)),
            pltpu.SemaphoreType.DMA((slots,)),
            pltpu.SemaphoreType.DMA((slots,)),
        ],
        compiler_params=pltpu.CompilerParams(
            collective_id=1, has_side_effects=True, vmem_limit_bytes=32 * 2**20
        ),
        cost_estimate=pl.CostEstimate(
            flops=2 * span * span * HD * slots * (slots + 1),
            bytes_accessed=8 * span * features,
            transcendentals=0,
        ),
        name="attend",
    )(windows, qkv)


def mix(factor, attn, state, gate, w_out, heads):
    rows, width = state.shape
    span, features = attn.shape
    chunks = width // COLS
    out = jax.ShapeDtypeStruct((rows, width), jnp.bfloat16)
    return pl.pallas_call(
        functools.partial(mix_kernel, heads),
        out_shape=(out, out),
        in_specs=[SMEM, VMEM, VMEM, VMEM, HBM],
        out_specs=(VMEM, VMEM),
        scratch_shapes=[
            pltpu.VMEM((chunks, features, COLS), jnp.bfloat16),
            pltpu.VMEM((chunks, span, COLS), jnp.bfloat16),
            pltpu.VMEM((chunks, heads - 1, rows, COLS), jnp.bfloat16),
            pltpu.SemaphoreType.DMA((chunks,)),
            pltpu.SemaphoreType.DMA((heads - 1, chunks)),
            pltpu.SemaphoreType.DMA((heads - 1, chunks)),
        ],
        compiler_params=pltpu.CompilerParams(
            collective_id=2, has_side_effects=True, vmem_limit_bytes=32 * 2**20
        ),
        cost_estimate=pl.CostEstimate(
            flops=2 * span * width * features,
            bytes_accessed=2 * width * features,
            transcendentals=0,
        ),
        name="mix",
    )(factor, attn, state, gate, w_out)


def shifted(array, axis, by):
    length = lax.axis_size(axis)
    pairs = [(i, i + by) for i in range(length) if 0 <= i + by < length]
    return lax.ppermute(array, axis, pairs)


def embed(times, width):
    half = width // 2
    freq = jnp.exp(-math.log(10000.0) * jnp.arange(half, dtype=jnp.float32) / half)
    angle = times[:, None] * freq[None, :]
    return jnp.concatenate([jnp.cos(angle), jnp.sin(angle)], axis=-1)


def absorb(carry, keys, values, first_row, queries, lower, slot, span):
    top, total, summed = carry
    count = keys.shape[0]
    heads_local = keys.shape[1] // HD
    key_heads = keys.reshape(count, heads_local, HD)
    value_heads = values.reshape(count, heads_local, HD)
    scores = jnp.einsum(
        "qhd,khd->hqk", queries, key_heads, preferred_element_type=jnp.float32
    ) / math.sqrt(HD)
    span_ids = (first_row + jnp.arange(count, dtype=jnp.int32)) // span
    valid = ((span_ids >= lower) & (span_ids <= slot))[None, None, :]
    masked = jnp.where(valid, scores, -1e30)
    new_top = jnp.maximum(top, jnp.max(masked, axis=-1))
    weights = jnp.where(valid, jnp.exp(scores - new_top[:, :, None]), 0.0)
    fade = jnp.exp(top - new_top)
    total = total * fade + jnp.sum(weights, axis=-1)
    summed = summed * fade[:, :, None] + jnp.einsum(
        "hqk,khd->hqd",
        weights.astype(jnp.bfloat16),
        value_heads,
        preferred_element_type=jnp.float32,
    )
    return (new_top, total, summed)


def on_device(
    latent,
    fresh,
    levels,
    windows,
    plan,
    mod_table,
    w_query,
    w_key,
    w_value,
    w_out,
    query_gain,
    key_gain,
):
    queue_count = lax.axis_size("queue")
    head_count = lax.axis_size("head")
    slot = lax.axis_index("queue")
    rows = latent.shape[0]
    span = rows * head_count
    features = w_query.shape[1]
    heads_local = features // HD
    table_hits = levels[:, None] == jnp.arange(plan.shape[0], dtype=jnp.int32)[None, :]
    t_all = jnp.sum(jnp.where(table_hits, plan[None, :], 0), axis=1).astype(jnp.float32)
    t_from = t_all[slot]
    t_to = jnp.where(slot > 0, t_all[jnp.maximum(slot - 1, 0)], 0.0)
    step_size = (t_to - t_from) / 1000.0
    lower = jnp.maximum(0, slot - windows[slot] + 1)
    emb = embed(t_from[None], latent.shape[1])[0]
    shift = mod_table[0] + emb
    scale = mod_table[1] + emb
    gate = mod_table[2] + emb
    state = latent
    speeds = []
    new = latent
    if queue_count == heads_local and latent.shape[1] % COLS == 0 and features % TILE == 0:
        for step in range(STEPS):
            qkv = project(
                state,
                shift[None],
                (1.0 + scale)[None],
                query_gain[None],
                key_gain[None],
                w_query,
                w_key,
                w_value,
                head_count,
            )
            attn = attend(windows, qkv, queue_count)
            speed, new = mix(step_size[None], attn, state, gate[None], w_out, head_count)
            speeds.append(speed)
            if step < STEPS - 1:
                moved = shifted(new, "queue", -1)
                state = jnp.where(slot == queue_count - 1, fresh, moved)
        return (jnp.stack(speeds), new)
    for step in range(STEPS):
        x = state.astype(jnp.float32)
        mean = jnp.mean(x, axis=-1, keepdims=True)
        var = jnp.mean((x - mean) ** 2, axis=-1, keepdims=True)
        normed = ((x - mean) * lax.rsqrt(var + 1e-06) * (1.0 + scale) + shift).astype(jnp.bfloat16)
        piece = lax.all_gather(normed, "head", axis=0, tiled=True)
        projected = jnp.concatenate(
            [
                jnp.dot(piece, w_query, preferred_element_type=jnp.float32),
                jnp.dot(piece, w_key, preferred_element_type=jnp.float32),
                jnp.dot(piece, w_value, preferred_element_type=jnp.float32),
            ],
            axis=-1,
        )
        q = projected[:, :features]
        k = projected[:, features : 2 * features]
        values = projected[:, 2 * features :].astype(jnp.bfloat16)
        query_sq, key_sq = lax.psum((jnp.sum(q * q, axis=-1), jnp.sum(k * k, axis=-1)), "head")
        every = features * head_count
        queries = (q * lax.rsqrt(query_sq / every + 1e-06)[:, None] * query_gain).astype(
            jnp.bfloat16
        )
        keys = (k * lax.rsqrt(key_sq / every + 1e-06)[:, None] * key_gain).astype(jnp.bfloat16)
        query_heads = queries.reshape(span, heads_local, HD)
        start_carry = (
            jnp.full((heads_local, span), -1e30, jnp.float32),
            jnp.zeros((heads_local, span), jnp.float32),
            jnp.zeros((heads_local, span, HD), jnp.float32),
        )
        inner = start_carry
        piece_keys = lax.all_gather(keys, "queue", axis=0, tiled=True)
        piece_values = lax.all_gather(values, "queue", axis=0, tiled=True)
        count = piece_keys.shape[0]
        blocks = count // span

        def one_block(running, block):
            block_keys, block_values, block_index = block
            return (
                absorb(
                    running,
                    block_keys,
                    block_values,
                    block_index * span,
                    query_heads,
                    lower,
                    slot,
                    span,
                ),
                None,
            )

        inner, unused = lax.scan(
            one_block,
            inner,
            (
                piece_keys.reshape(blocks, span, features),
                piece_values.reshape(blocks, span, features),
                jnp.arange(blocks, dtype=jnp.int32),
            ),
        )
        top, total, summed = inner
        attn = (
            jnp.transpose(summed / total[:, :, None], (1, 0, 2))
            .reshape(span, features)
            .astype(jnp.bfloat16)
        )
        mixed = lax.psum_scatter(
            jnp.dot(attn, w_out, preferred_element_type=jnp.float32).astype(jnp.bfloat16),
            "head",
            scatter_dimension=0,
            tiled=True,
        ).astype(jnp.float32)
        speed = (x + gate * mixed).astype(jnp.bfloat16)
        speeds.append(speed)
        new = (x + step_size * speed.astype(jnp.float32)).astype(jnp.bfloat16)
        if step < STEPS - 1:
            moved = shifted(new, "queue", -1)
            state = jnp.where(slot == queue_count - 1, fresh, moved)
    return (jnp.stack(speeds), new)


def solution(mesh):
    return jax.shard_map(
        on_device,
        mesh=mesh,
        in_specs=(
            P(("queue", "head"), None),
            P("head", None),
            P(),
            P(),
            P(),
            P(),
            P(None, "head"),
            P(None, "head"),
            P(None, "head"),
            P("head", None),
            P("head"),
            P("head"),
        ),
        out_specs=(P(None, ("queue", "head"), None), P(("queue", "head"), None)),
        check_vma=False,
    )
```

```python
import functools
import math

import jax
import jax.numpy as jnp
from jax import lax
from jax.experimental import pallas as pl
from jax.experimental.pallas import tpu as pltpu
from jax.sharding import PartitionSpec as P

HD = 128
STEPS = 2
COLS = 1024
TILE = 512
MESH = pl.DeviceIdType.MESH
VMEM = pl.BlockSpec(memory_space=pltpu.VMEM)
SMEM = pl.BlockSpec(memory_space=pltpu.SMEM)
HBM = pl.BlockSpec(memory_space=pl.ANY)


def fused_kernel(
    slots,
    heads,
    levels_ref,
    windows_ref,
    plan_ref,
    latent_ref,
    fresh_ref,
    table_ref,
    wq_ref,
    wk_ref,
    wv_ref,
    wo_ref,
    gq_ref,
    gk_ref,
    speed_ref,
    new_ref,
    state,
    mod,
    weights,
    outer,
    gathered,
    acc,
    sums,
    sums_in,
    qkv,
    held,
    results,
    attn,
    sent,
    got,
    relay,
    in_sem,
    w_sem,
    o_sem,
    own_send,
    own_recv,
    fwd_send,
    fwd_recv,
    sum_send,
    sum_recv,
    v_send,
    v_recv,
    qk_send,
    qk_recv,
    local_sem,
    back_send,
    back_recv,
    part_send,
    part_recv,
    shift_send,
    shift_recv,
):
    slot_me = lax.axis_index("queue")
    me = lax.axis_index("head")
    across = me + 1 - 2 * lax.rem(me, 2)
    along = lax.rem(me + 2, heads)
    near = (across, along)
    far = lax.rem(across + 2, heads)
    rows, width = state.shape[1:]
    chunks, span = gathered.shape[:2]
    features = wq_ref.shape[1]
    heads_local = features // HD
    sources = (wq_ref, wk_ref, wv_ref)

    def block(owner):
        return pl.ds(pl.multiple_of(owner * rows, rows), rows)

    def cols(c):
        return slice(c * COLS, (c + 1) * COLS)

    def half(s):
        return pl.ds(s * TILE, TILE)

    load = pltpu.make_async_copy(latent_ref, state.at[0], in_sem.at[0])
    load_fresh = pltpu.make_async_copy(fresh_ref, state.at[1], in_sem.at[1])
    load.start()

    def fetch(c, m):
        at = pl.ds(c * COLS, COLS)
        return pltpu.make_async_copy(
            sources[m].at[at, :], weights.at[m, at, :], w_sem.at[c, m]
        )

    def fetch_outer(c):
        return pltpu.make_async_copy(
            wo_ref.at[:, pl.ds(c * COLS, COLS)], outer.at[c], o_sem.at[c]
        )

    for c in range(chunks):
        for m in range(3):
            fetch(c, m).start()
    for c in range(chunks):
        fetch_outer(c).start()

    @pl.when(slot_me == slots - 1)
    def _():
        load_fresh.start()

    barrier = pltpu.get_barrier_semaphore()
    for d in range(1, heads):
        pl.semaphore_signal(
            barrier, inc=1, device_id={"head": lax.rem(me + d, heads)}, device_id_type=MESH
        )
    for d in range(1, slots):
        pl.semaphore_signal(
            barrier, inc=1, device_id={"queue": lax.rem(slot_me + d, slots)}, device_id_type=MESH
        )

    t_from = plan_ref[levels_ref[slot_me]].astype(jnp.float32)
    t_below = plan_ref[levels_ref[jnp.maximum(slot_me - 1, 0)]].astype(jnp.float32)
    t_to = jnp.where(slot_me > 0, t_below, 0.0)
    factor = (t_to - t_from) / 1000.0
    mid = width // 2
    index = lax.broadcasted_iota(jnp.int32, (1, mid), 1).astype(jnp.float32)
    angle = t_from * jnp.exp(-math.log(10000.0) * index / mid)
    for at, emb in ((slice(0, mid), jnp.cos(angle)), (slice(mid, width), jnp.sin(angle))):
        mod[0:1, at] = table_ref[0:1, at] + emb
        mod[1:2, at] = 1.0 + (table_ref[1:2, at] + emb)
        mod[2:3, at] = table_ref[2:3, at] + emb

    pl.semaphore_wait(barrier, heads - 1 + slots - 1)
    load.wait()

    def own(c, way, owner):
        part = gathered.at[c, block(owner), :]
        return pltpu.make_async_remote_copy(
            src_ref=part,
            dst_ref=part,
            send_sem=own_send.at[c, way],
            recv_sem=own_recv.at[c, way],
            device_id={"head": near[way]},
            device_id_type=MESH,
        )

    def forward(c, s, owner):
        part = gathered.at[c, block(owner), half(s)]
        return pltpu.make_async_remote_copy(
            src_ref=part,
            dst_ref=part,
            send_sem=fwd_send.at[c, s],
            recv_sem=fwd_recv.at[c, s],
            device_id={"head": near[1 - s]},
            device_id_type=MESH,
        )

    def share(d):
        return pltpu.make_async_remote_copy(
            src_ref=sums,
            dst_ref=sums_in.at[d - 1],
            send_sem=sum_send.at[d - 1],
            recv_sem=sum_recv.at[d - 1],
            device_id={"head": lax.rem(me + d, heads)},
            device_id_type=MESH,
        )

    def multiply(c, m):
        def tile(n, carry):
            at = pl.ds(pl.multiple_of(n * TILE, TILE), TILE)
            product = jnp.dot(
                gathered[c],
                weights[m, pl.ds(c * COLS, COLS), at],
                preferred_element_type=jnp.float32,
            )
            acc[m, :, at] = product if c == 0 else acc[m, :, at] + product
            return carry

        lax.fori_loop(0, features // TILE, tile, 0)

    def rows_of(slot):
        return pl.ds(pl.multiple_of(slot * span, span), span)

    def columns_of(head):
        return pl.ds(pl.multiple_of(head * HD, HD), HD)

    def push_v(step, peer, owner):
        return pltpu.make_async_remote_copy(
            src_ref=qkv.at[peer, 2],
            dst_ref=held.at[step, 2, rows_of(owner), :],
            send_sem=v_send.at[step, peer],
            recv_sem=v_recv.at[step, owner],
            device_id={"queue": peer},
            device_id_type=MESH,
        )

    def push_qk(step, peer, owner):
        return pltpu.make_async_remote_copy(
            src_ref=qkv.at[peer, 0:2],
            dst_ref=held.at[step, 0:2, rows_of(owner), :],
            send_sem=qk_send.at[step, peer],
            recv_sem=qk_recv.at[step, owner],
            device_id={"queue": peer},
            device_id_type=MESH,
        )

    def give(step, peer, head):
        return pltpu.make_async_remote_copy(
            src_ref=results.at[peer],
            dst_ref=attn.at[:, columns_of(head)],
            send_sem=back_send.at[step, peer],
            recv_sem=back_recv.at[step, head],
            device_id={"queue": peer},
            device_id_type=MESH,
        )

    def part(c, s, kind):
        target = near[s] if kind < 2 else near[1 - s]
        if kind == 0:
            source = sent.at[c, block(far), half(s)]
        elif kind == 1:
            source = sent.at[c, block(near[s]), half(s)]
        else:
            source = relay.at[c, s]
        return pltpu.make_async_remote_copy(
            src_ref=source,
            dst_ref=got.at[c, s, kind],
            send_sem=part_send.at[c, s, kind],
            recv_sem=part_recv.at[c, s, kind],
            device_id={"head": target},
            device_id_type=MESH,
        )

    def hand_down(c, peer):
        at = pl.ds(c * COLS, COLS)
        return pltpu.make_async_remote_copy(
            src_ref=new_ref.at[:, at],
            dst_ref=state.at[1, :, at],
            send_sem=shift_send.at[c],
            recv_sem=shift_recv.at[c],
            device_id={"queue": peer},
            device_id_type=MESH,
        )

    above = lax.rem(slot_me + 1, slots)
    below = lax.rem(slot_me + slots - 1, slots)

    for step in range(STEPS):
        x = state[step].astype(jnp.float32)
        mean = jnp.mean(x, axis=-1, keepdims=True)
        var = jnp.mean((x - mean) ** 2, axis=-1, keepdims=True)
        inv = lax.rsqrt(var + 1e-06)
        for c in range(chunks):
            piece = state[step, :, cols(c)].astype(jnp.float32)
            normed = (piece - mean) * inv * mod[1:2, cols(c)] + mod[0:1, cols(c)]
            gathered[c, block(me), :] = normed.astype(jnp.bfloat16)
            if c < 2:
                own(c, 0, me).start()
                own(c, 1, me).start()
        for c in range(chunks):
            own(c, 0, across).wait_recv()
            forward(c, 0, across).start()
            own(c, 1, along).wait_recv()
            forward(c, 1, along).start()
            if c + 2 < chunks:
                own(c + 2, 0, me).start()
                own(c + 2, 1, me).start()
            if c > 0:
                forward(c - 1, 0, far).wait_recv()
                forward(c - 1, 1, far).wait_recv()
                for m in range(3):
                    if step == 0:
                        fetch(c - 1, m).wait()
                    multiply(c - 1, m)
        last = chunks - 1
        forward(last, 0, far).wait_recv()
        forward(last, 1, far).wait_recv()
        for m in range(2):
            if step == 0:
                fetch(last, m).wait()
            multiply(last, m)
            value = acc[m]
            total = jnp.sum(value * value, axis=-1, keepdims=True)
            wide = jnp.broadcast_to(total, (span, HD))
            for k in range(span // HD):
                turned = jnp.transpose(wide[k * HD : (k + 1) * HD])
                sums[m, :, k * HD : (k + 1) * HD] = turned[:8]
        for d in range(1, heads):
            share(d).start()
        if step == 0:
            fetch(last, 2).wait()
        multiply(last, 2)
        for j in range(heads_local):
            qkv[j, 2] = acc[2, :, j * HD : (j + 1) * HD].astype(jnp.bfloat16)
        for d in range(1, slots):
            push_v(step, lax.rem(slot_me + d, slots), slot_me).start()
        for d in range(1, heads):
            share(d).wait_recv()
        for m, gain_ref in ((0, gq_ref), (1, gk_ref)):
            total = sums[m]
            for d in range(1, heads):
                total = total + sums_in[d - 1, m]
            norm = lax.rsqrt(total / (features * heads) + 1e-06)
            pieces = []
            for k in range(span // HD):
                row = norm[:1, k * HD : (k + 1) * HD]
                pieces.append(jnp.transpose(jnp.broadcast_to(row, (HD, HD))))
            column = jnp.concatenate(pieces, axis=0) if len(pieces) > 1 else pieces[0]
            for j in range(heads_local):
                at = slice(j * HD, (j + 1) * HD)
                qkv[j, m] = (acc[m, :, at] * column * gain_ref[:, at]).astype(jnp.bfloat16)
        for d in range(1, slots):
            push_qk(step, lax.rem(slot_me + d, slots), slot_me).start()
        keep = pltpu.make_async_copy(
            qkv.at[slot_me], held.at[step, :, rows_of(slot_me), :], local_sem.at[0]
        )
        keep.start()
        for d in range(1, heads):
            share(d).wait_send()
        for c in range(chunks):
            for s in range(2):
                own(c, s, me).wait_send()
                forward(c, s, near[s]).wait_send()
        keep.wait()

        settle = pltpu.make_async_copy(
            results.at[slot_me], attn.at[:, columns_of(slot_me)], local_sem.at[1]
        )
        for slot in range(slots):

            @pl.when(slot_me != slot)
            def _(slot=slot):
                push_v(step, slot, slot).wait_recv()
                push_qk(step, slot, slot).wait_recv()

            count = (slot + 1) * span
            scores = lax.dot_general(
                held[step, 0, slot * span : count, :],
                held[step, 1, :count, :],
                (((1,), (1,)), ((), ())),
                preferred_element_type=jnp.float32,
            ) * (1.0 / math.sqrt(HD))
            ids = lax.broadcasted_iota(jnp.int32, (1, count), 1)
            valid = ids >= (slot - windows_ref[slot] + 1) * span
            masked = jnp.where(valid, scores, -1e30)
            top = jnp.max(masked, axis=-1, keepdims=True)
            soft = jnp.exp(masked - top)
            total = jnp.sum(soft, axis=-1, keepdims=True)
            summed = jnp.dot(
                soft.astype(jnp.bfloat16),
                held[step, 2, :count, :],
                preferred_element_type=jnp.float32,
            )
            results[slot] = (summed / total).astype(jnp.bfloat16)

            @pl.when(slot_me != slot)
            def _(slot=slot):
                give(step, slot, slot_me).start()

            @pl.when(slot_me == slot)
            def _():
                settle.start()

        settle.wait()
        for slot in range(slots):

            @pl.when(slot_me != slot)
            def _(slot=slot):
                give(step, slot, slot).wait_recv()

        def relay_part(c):
            for s in range(2):
                part(c, s, 0).wait_recv()
                both = sent[c, block(near[1 - s]), half(s)].astype(jnp.float32) + got[
                    c, s, 0
                ].astype(jnp.float32)
                relay[c, s] = both.astype(jnp.bfloat16)
                part(c, s, 2).start()

        def finish(c):
            for s in range(2):
                at = slice(c * COLS + s * TILE, c * COLS + (s + 1) * TILE)
                part(c, s, 1).wait_recv()
                part(c, s, 2).wait_recv()
                total = (
                    sent[c, block(me), half(s)].astype(jnp.float32)
                    + got[c, s, 1].astype(jnp.float32)
                    + got[c, s, 2].astype(jnp.float32)
                )
                before = state[step, :, at].astype(jnp.float32)
                speed = (before + mod[2:3, at] * total).astype(jnp.bfloat16)
                speed_ref[step, :, at] = speed
                new_ref[:, at] = (before + factor * speed.astype(jnp.float32)).astype(
                    jnp.bfloat16
                )
            if step < STEPS - 1:

                @pl.when(slot_me > 0)
                def _():
                    hand_down(c, below).start()

        for c in range(chunks):
            if step == 0:
                fetch_outer(c).wait()
            for s in range(2):
                sent[c, :, s * TILE : (s + 1) * TILE] = jnp.dot(
                    attn[...],
                    outer[c, :, s * TILE : (s + 1) * TILE],
                    preferred_element_type=jnp.float32,
                ).astype(jnp.bfloat16)
                part(c, s, 0).start()
                part(c, s, 1).start()
            if c > 0:
                relay_part(c - 1)
            if c > 1:
                finish(c - 2)
        relay_part(last)
        if last > 0:
            finish(last - 1)
        finish(last)
        for c in range(chunks):
            for s in range(2):
                for kind in range(3):
                    part(c, s, kind).wait_send()
        for slot in range(slots):

            @pl.when(slot_me != slot)
            def _(slot=slot):
                push_v(step, slot, slot_me).wait_send()
                push_qk(step, slot, slot_me).wait_send()
                give(step, slot, slot_me).wait_send()

        if step < STEPS - 1:

            @pl.when(slot_me > 0)
            def _():
                for c in range(chunks):
                    hand_down(c, below).wait_send()

            @pl.when(slot_me < slots - 1)
            def _():
                for c in range(chunks):
                    hand_down(c, above).wait_recv()

            @pl.when(slot_me == slots - 1)
            def _():
                load_fresh.wait()


def fused(
    latent, fresh, levels, windows, plan, table, wq, wk, wv, wo, gq, gk, slots, heads
):
    rows, width = latent.shape
    span, features = rows * heads, wq.shape[1]
    chunks, heads_local = width // COLS, features // HD
    dma = pltpu.SemaphoreType.DMA
    bf16, f32 = jnp.bfloat16, jnp.float32
    return pl.pallas_call(
        functools.partial(fused_kernel, slots, heads),
        out_shape=(
            jax.ShapeDtypeStruct((STEPS, rows, width), bf16),
            jax.ShapeDtypeStruct((rows, width), bf16),
        ),
        in_specs=[SMEM] * 3 + [HBM] * 2 + [VMEM] + [HBM] * 4 + [VMEM] * 2,
        out_specs=(VMEM, VMEM),
        scratch_shapes=[
            pltpu.VMEM((STEPS, rows, width), bf16),
            pltpu.VMEM((3, width), f32),
            pltpu.VMEM((3, width, features), bf16),
            pltpu.VMEM((chunks, features, COLS), bf16),
            pltpu.VMEM((chunks, span, COLS), bf16),
            pltpu.VMEM((3, span, features), f32),
            pltpu.VMEM((2, 8, span), f32),
            pltpu.VMEM((heads - 1, 2, 8, span), f32),
            pltpu.VMEM((heads_local, 3, span, HD), bf16),
            pltpu.VMEM((STEPS, 3, slots * span, HD), bf16),
            pltpu.VMEM((slots, span, HD), bf16),
            pltpu.VMEM((span, features), bf16),
            pltpu.VMEM((chunks, span, COLS), bf16),
            pltpu.VMEM((chunks, 2, 3, rows, TILE), bf16),
            pltpu.VMEM((chunks, 2, rows, TILE), bf16),
            dma((2,)),
            dma((chunks, 3)),
            dma((chunks,)),
            dma((chunks, 2)),
            dma((chunks, 2)),
            dma((chunks, 2)),
            dma((chunks, 2)),
            dma((heads - 1,)),
            dma((heads - 1,)),
            dma((STEPS, slots)),
            dma((STEPS, slots)),
            dma((STEPS, slots)),
            dma((STEPS, slots)),
            dma((2,)),
            dma((STEPS, slots)),
            dma((STEPS, slots)),
            dma((chunks, 2, 3)),
            dma((chunks, 2, 3)),
            dma((chunks,)),
            dma((chunks,)),
        ],
        compiler_params=pltpu.CompilerParams(
            collective_id=0, has_side_effects=True, vmem_limit_bytes=58 * 2**20
        ),
        cost_estimate=pl.CostEstimate(
            flops=STEPS * 8 * span * width * features,
            bytes_accessed=8 * width * features,
            transcendentals=0,
        ),
        name="denoise",
    )(levels, windows, plan, latent, fresh, table, wq, wk, wv, wo, gq, gk)


def shifted(array, axis, by):
    length = lax.axis_size(axis)
    pairs = [(i, i + by) for i in range(length) if 0 <= i + by < length]
    return lax.ppermute(array, axis, pairs)


def embed(times, width):
    half = width // 2
    freq = jnp.exp(-math.log(10000.0) * jnp.arange(half, dtype=jnp.float32) / half)
    angle = times[:, None] * freq[None, :]
    return jnp.concatenate([jnp.cos(angle), jnp.sin(angle)], axis=-1)


def absorb(carry, keys, values, first_row, queries, lower, slot, span):
    top, total, summed = carry
    count = keys.shape[0]
    heads_local = keys.shape[1] // HD
    key_heads = keys.reshape(count, heads_local, HD)
    value_heads = values.reshape(count, heads_local, HD)
    scores = jnp.einsum(
        "qhd,khd->hqk", queries, key_heads, preferred_element_type=jnp.float32
    ) / math.sqrt(HD)
    span_ids = (first_row + jnp.arange(count, dtype=jnp.int32)) // span
    valid = ((span_ids >= lower) & (span_ids <= slot))[None, None, :]
    masked = jnp.where(valid, scores, -1e30)
    new_top = jnp.maximum(top, jnp.max(masked, axis=-1))
    weights = jnp.where(valid, jnp.exp(scores - new_top[:, :, None]), 0.0)
    fade = jnp.exp(top - new_top)
    total = total * fade + jnp.sum(weights, axis=-1)
    summed = summed * fade[:, :, None] + jnp.einsum(
        "hqk,khd->hqd",
        weights.astype(jnp.bfloat16),
        value_heads,
        preferred_element_type=jnp.float32,
    )
    return (new_top, total, summed)


def on_device(
    latent,
    fresh,
    levels,
    windows,
    plan,
    mod_table,
    w_query,
    w_key,
    w_value,
    w_out,
    query_gain,
    key_gain,
):
    queue_count = lax.axis_size("queue")
    head_count = lax.axis_size("head")
    slot = lax.axis_index("queue")
    rows = latent.shape[0]
    span = rows * head_count
    features = w_query.shape[1]
    heads_local = features // HD
    fits = latent.shape[1] % COLS == 0 and features % TILE == 0 and COLS == 2 * TILE
    if queue_count == heads_local and head_count == 4 and span == HD and fits:
        return fused(
            latent,
            fresh,
            levels,
            windows,
            plan,
            mod_table,
            w_query,
            w_key,
            w_value,
            w_out,
            query_gain[None],
            key_gain[None],
            queue_count,
            head_count,
        )
    table_hits = levels[:, None] == jnp.arange(plan.shape[0], dtype=jnp.int32)[None, :]
    t_all = jnp.sum(jnp.where(table_hits, plan[None, :], 0), axis=1).astype(jnp.float32)
    t_from = t_all[slot]
    t_to = jnp.where(slot > 0, t_all[jnp.maximum(slot - 1, 0)], 0.0)
    step_size = (t_to - t_from) / 1000.0
    lower = jnp.maximum(0, slot - windows[slot] + 1)
    emb = embed(t_from[None], latent.shape[1])[0]
    shift = mod_table[0] + emb
    scale = mod_table[1] + emb
    gate = mod_table[2] + emb
    state = latent
    speeds = []
    new = latent
    for step in range(STEPS):
        x = state.astype(jnp.float32)
        mean = jnp.mean(x, axis=-1, keepdims=True)
        var = jnp.mean((x - mean) ** 2, axis=-1, keepdims=True)
        normed = ((x - mean) * lax.rsqrt(var + 1e-06) * (1.0 + scale) + shift).astype(jnp.bfloat16)
        piece = lax.all_gather(normed, "head", axis=0, tiled=True)
        projected = jnp.concatenate(
            [
                jnp.dot(piece, w_query, preferred_element_type=jnp.float32),
                jnp.dot(piece, w_key, preferred_element_type=jnp.float32),
                jnp.dot(piece, w_value, preferred_element_type=jnp.float32),
            ],
            axis=-1,
        )
        q = projected[:, :features]
        k = projected[:, features : 2 * features]
        values = projected[:, 2 * features :].astype(jnp.bfloat16)
        query_sq, key_sq = lax.psum((jnp.sum(q * q, axis=-1), jnp.sum(k * k, axis=-1)), "head")
        every = features * head_count
        queries = (q * lax.rsqrt(query_sq / every + 1e-06)[:, None] * query_gain).astype(
            jnp.bfloat16
        )
        keys = (k * lax.rsqrt(key_sq / every + 1e-06)[:, None] * key_gain).astype(jnp.bfloat16)
        query_heads = queries.reshape(span, heads_local, HD)
        start_carry = (
            jnp.full((heads_local, span), -1e30, jnp.float32),
            jnp.zeros((heads_local, span), jnp.float32),
            jnp.zeros((heads_local, span, HD), jnp.float32),
        )
        inner = start_carry
        piece_keys = lax.all_gather(keys, "queue", axis=0, tiled=True)
        piece_values = lax.all_gather(values, "queue", axis=0, tiled=True)
        count = piece_keys.shape[0]
        blocks = count // span

        def one_block(running, block):
            block_keys, block_values, block_index = block
            return (
                absorb(
                    running,
                    block_keys,
                    block_values,
                    block_index * span,
                    query_heads,
                    lower,
                    slot,
                    span,
                ),
                None,
            )

        inner, unused = lax.scan(
            one_block,
            inner,
            (
                piece_keys.reshape(blocks, span, features),
                piece_values.reshape(blocks, span, features),
                jnp.arange(blocks, dtype=jnp.int32),
            ),
        )
        top, total, summed = inner
        attn = (
            jnp.transpose(summed / total[:, :, None], (1, 0, 2))
            .reshape(span, features)
            .astype(jnp.bfloat16)
        )
        mixed = lax.psum_scatter(
            jnp.dot(attn, w_out, preferred_element_type=jnp.float32).astype(jnp.bfloat16),
            "head",
            scatter_dimension=0,
            tiled=True,
        ).astype(jnp.float32)
        speed = (x + gate * mixed).astype(jnp.bfloat16)
        speeds.append(speed)
        new = (x + step_size * speed.astype(jnp.float32)).astype(jnp.bfloat16)
        if step < STEPS - 1:
            moved = shifted(new, "queue", -1)
            state = jnp.where(slot == queue_count - 1, fresh, moved)
    return (jnp.stack(speeds), new)


def solution(mesh):
    return jax.shard_map(
        on_device,
        mesh=mesh,
        in_specs=(
            P(("queue", "head"), None),
            P("head", None),
            P(),
            P(),
            P(),
            P(),
            P(None, "head"),
            P(None, "head"),
            P(None, "head"),
            P("head", None),
            P("head"),
            P("head"),
        ),
        out_specs=(P(None, ("queue", "head"), None), P(("queue", "head"), None)),
        check_vma=False,
    )
```

```python
import functools
import math

import jax
import jax.numpy as jnp
from jax import lax
from jax.experimental import pallas as pl
from jax.experimental.pallas import tpu as pltpu
from jax.sharding import PartitionSpec as P

HD = 128
STEPS = 2
COLS = 1024
TILE = 512
MESH = pl.DeviceIdType.MESH
VMEM = pl.BlockSpec(memory_space=pltpu.VMEM)
SMEM = pl.BlockSpec(memory_space=pltpu.SMEM)
HBM = pl.BlockSpec(memory_space=pl.ANY)


def fused_kernel(
    slots,
    heads,
    levels_ref,
    windows_ref,
    plan_ref,
    latent_ref,
    fresh_ref,
    table_ref,
    wq_ref,
    wk_ref,
    wv_ref,
    wo_ref,
    gq_ref,
    gk_ref,
    speed_ref,
    new_ref,
    state,
    mod,
    weights,
    outer,
    gathered,
    acc,
    sums,
    sums_in,
    qkv,
    held,
    results,
    attn,
    sent,
    got,
    relay,
    in_sem,
    w_sem,
    o_sem,
    own_send,
    own_recv,
    fwd_send,
    fwd_recv,
    sum_send,
    sum_recv,
    v_send,
    v_recv,
    qk_send,
    qk_recv,
    local_sem,
    back_send,
    back_recv,
    part_send,
    part_recv,
    shift_send,
    shift_recv,
):
    slot_me = lax.axis_index("queue")
    me = lax.axis_index("head")
    across = me + 1 - 2 * lax.rem(me, 2)
    along = lax.rem(me + 2, heads)
    near = (across, along)
    far = lax.rem(across + 2, heads)
    rows, width = state.shape[1:]
    chunks, span = gathered.shape[:2]
    features = wq_ref.shape[1]
    heads_local = features // HD
    sources = (wq_ref, wk_ref, wv_ref)

    def block(owner):
        return pl.ds(pl.multiple_of(owner * rows, rows), rows)

    def cols(c):
        return slice(c * COLS, (c + 1) * COLS)

    def half(s):
        return pl.ds(s * TILE, TILE)

    load = pltpu.make_async_copy(latent_ref, state.at[0], in_sem.at[0])
    load_fresh = pltpu.make_async_copy(fresh_ref, state.at[1], in_sem.at[1])
    load.start()

    def fetch(c, m):
        at = pl.ds(c * COLS, COLS)
        return pltpu.make_async_copy(
            sources[m].at[at, :], weights.at[m, at, :], w_sem.at[c, m]
        )

    def fetch_outer(c):
        return pltpu.make_async_copy(
            wo_ref.at[:, pl.ds(c * COLS, COLS)], outer.at[c], o_sem.at[c]
        )

    for c in range(chunks):
        for m in range(3):
            fetch(c, m).start()
    for c in range(chunks):
        fetch_outer(c).start()

    @pl.when(slot_me == slots - 1)
    def _():
        load_fresh.start()

    barrier = pltpu.get_barrier_semaphore()
    for d in range(1, heads):
        pl.semaphore_signal(
            barrier, inc=1, device_id={"head": lax.rem(me + d, heads)}, device_id_type=MESH
        )
    for d in range(1, slots):
        pl.semaphore_signal(
            barrier, inc=1, device_id={"queue": lax.rem(slot_me + d, slots)}, device_id_type=MESH
        )

    t_from = plan_ref[levels_ref[slot_me]].astype(jnp.float32)
    t_below = plan_ref[levels_ref[jnp.maximum(slot_me - 1, 0)]].astype(jnp.float32)
    t_to = jnp.where(slot_me > 0, t_below, 0.0)
    factor = (t_to - t_from) / 1000.0
    mid = width // 2
    index = lax.broadcasted_iota(jnp.int32, (1, mid), 1).astype(jnp.float32)
    angle = t_from * jnp.exp(-math.log(10000.0) * index / mid)
    for at, emb in ((slice(0, mid), jnp.cos(angle)), (slice(mid, width), jnp.sin(angle))):
        mod[0:1, at] = table_ref[0:1, at] + emb
        mod[1:2, at] = 1.0 + (table_ref[1:2, at] + emb)
        mod[2:3, at] = table_ref[2:3, at] + emb

    pl.semaphore_wait(barrier, heads - 1 + slots - 1)
    load.wait()

    def own(c, way, owner):
        part = gathered.at[c, block(owner), :]
        return pltpu.make_async_remote_copy(
            src_ref=part,
            dst_ref=part,
            send_sem=own_send.at[c, way],
            recv_sem=own_recv.at[c, way],
            device_id={"head": near[way]},
            device_id_type=MESH,
        )

    def forward(c, s, owner):
        part = gathered.at[c, block(owner), half(s)]
        return pltpu.make_async_remote_copy(
            src_ref=part,
            dst_ref=part,
            send_sem=fwd_send.at[c, s],
            recv_sem=fwd_recv.at[c, s],
            device_id={"head": near[1 - s]},
            device_id_type=MESH,
        )

    def share(d):
        return pltpu.make_async_remote_copy(
            src_ref=sums,
            dst_ref=sums_in.at[d - 1],
            send_sem=sum_send.at[d - 1],
            recv_sem=sum_recv.at[d - 1],
            device_id={"head": lax.rem(me + d, heads)},
            device_id_type=MESH,
        )

    def multiply(c, first, end):
        def one(m, carry):
            product = jnp.dot(
                gathered[c],
                weights[m, c * COLS : (c + 1) * COLS, :],
                preferred_element_type=jnp.float32,
            )
            acc[m] = product if c == 0 else acc[m] + product
            return carry

        lax.fori_loop(first, end, one, 0)

    def rows_of(slot):
        return pl.ds(pl.multiple_of(slot * span, span), span)

    def columns_of(head):
        return pl.ds(pl.multiple_of(head * HD, HD), HD)

    def push_v(step, peer, owner):
        return pltpu.make_async_remote_copy(
            src_ref=qkv.at[peer, 2],
            dst_ref=held.at[step, 2, rows_of(owner), :],
            send_sem=v_send.at[step, peer],
            recv_sem=v_recv.at[step, owner],
            device_id={"queue": peer},
            device_id_type=MESH,
        )

    def push_qk(step, peer, owner):
        return pltpu.make_async_remote_copy(
            src_ref=qkv.at[peer, 0:2],
            dst_ref=held.at[step, 0:2, rows_of(owner), :],
            send_sem=qk_send.at[step, peer],
            recv_sem=qk_recv.at[step, owner],
            device_id={"queue": peer},
            device_id_type=MESH,
        )

    def give(step, peer, head):
        return pltpu.make_async_remote_copy(
            src_ref=results.at[peer],
            dst_ref=attn.at[:, columns_of(head)],
            send_sem=back_send.at[step, peer],
            recv_sem=back_recv.at[step, head],
            device_id={"queue": peer},
            device_id_type=MESH,
        )

    def part(c, s, kind):
        target = near[s] if kind < 2 else near[1 - s]
        if kind == 0:
            source = sent.at[c, block(far), half(s)]
        elif kind == 1:
            source = sent.at[c, block(near[s]), half(s)]
        else:
            source = relay.at[c, s]
        return pltpu.make_async_remote_copy(
            src_ref=source,
            dst_ref=got.at[c, s, kind],
            send_sem=part_send.at[c, s, kind],
            recv_sem=part_recv.at[c, s, kind],
            device_id={"head": target},
            device_id_type=MESH,
        )

    def hand_down(c, peer):
        at = pl.ds(c * COLS, COLS)
        return pltpu.make_async_remote_copy(
            src_ref=new_ref.at[:, at],
            dst_ref=state.at[1, :, at],
            send_sem=shift_send.at[c],
            recv_sem=shift_recv.at[c],
            device_id={"queue": peer},
            device_id_type=MESH,
        )

    above = lax.rem(slot_me + 1, slots)
    below = lax.rem(slot_me + slots - 1, slots)

    for step in range(STEPS):
        x = state[step].astype(jnp.float32)
        mean = jnp.mean(x, axis=-1, keepdims=True)
        var = jnp.mean((x - mean) ** 2, axis=-1, keepdims=True)
        inv = lax.rsqrt(var + 1e-06)
        for c in range(chunks):
            piece = state[step, :, cols(c)].astype(jnp.float32)
            normed = (piece - mean) * inv * mod[1:2, cols(c)] + mod[0:1, cols(c)]
            gathered[c, block(me), :] = normed.astype(jnp.bfloat16)
            if c < 2:
                own(c, 0, me).start()
                own(c, 1, me).start()
        for c in range(chunks):
            own(c, 0, across).wait_recv()
            forward(c, 0, across).start()
            own(c, 1, along).wait_recv()
            forward(c, 1, along).start()
            if c + 2 < chunks:
                own(c + 2, 0, me).start()
                own(c + 2, 1, me).start()
            if c > 0:
                forward(c - 1, 0, far).wait_recv()
                forward(c - 1, 1, far).wait_recv()
                if step == 0:
                    for m in range(3):
                        fetch(c - 1, m).wait()
                multiply(c - 1, 0, 3)
        last = chunks - 1
        forward(last, 0, far).wait_recv()
        forward(last, 1, far).wait_recv()
        if step == 0:
            for m in range(3):
                fetch(last, m).wait()
        multiply(last, 0, 2)
        for m in range(2):
            value = acc[m]
            total = jnp.sum(value * value, axis=-1, keepdims=True)
            wide = jnp.broadcast_to(total, (span, HD))
            for k in range(span // HD):
                turned = jnp.transpose(wide[k * HD : (k + 1) * HD])
                sums[m, :, k * HD : (k + 1) * HD] = turned[:8]
        for d in range(1, heads):
            share(d).start()
        multiply(last, 2, 3)
        for j in range(heads_local):
            qkv[j, 2] = acc[2, :, j * HD : (j + 1) * HD].astype(jnp.bfloat16)
        for d in range(1, slots):
            push_v(step, lax.rem(slot_me + slots - d, slots), slot_me).start()
        for d in range(1, heads):
            share(d).wait_recv()
        for m, gain_ref in ((0, gq_ref), (1, gk_ref)):
            total = sums[m]
            for d in range(1, heads):
                total = total + sums_in[d - 1, m]
            norm = lax.rsqrt(total / (features * heads) + 1e-06)
            if m == 0:
                norm = norm * (1.0 / (math.log(2.0) * math.sqrt(HD)))
            pieces = []
            for k in range(span // HD):
                row = norm[:1, k * HD : (k + 1) * HD]
                pieces.append(jnp.transpose(jnp.broadcast_to(row, (HD, HD))))
            column = jnp.concatenate(pieces, axis=0) if len(pieces) > 1 else pieces[0]
            for j in range(heads_local):
                at = slice(j * HD, (j + 1) * HD)
                qkv[j, m] = (acc[m, :, at] * column * gain_ref[:, at]).astype(jnp.bfloat16)
        for d in range(1, slots):
            push_qk(step, lax.rem(slot_me + slots - d, slots), slot_me).start()
        keep = pltpu.make_async_copy(
            qkv.at[slot_me], held.at[step, :, rows_of(slot_me), :], local_sem.at[0]
        )
        keep.start()
        for d in range(1, heads):
            share(d).wait_send()
        for c in range(chunks):
            for s in range(2):
                own(c, s, me).wait_send()
                forward(c, s, near[s]).wait_send()
        keep.wait()

        settle = pltpu.make_async_copy(
            results.at[slot_me], attn.at[:, columns_of(slot_me)], local_sem.at[1]
        )
        for pair in range(0, slots, 2):
            group = range(pair, min(pair + 2, slots))
            for slot in group:

                @pl.when(slot_me != slot)
                def _(slot=slot):
                    push_v(step, slot, slot).wait_recv()
                    push_qk(step, slot, slot).wait_recv()

            end = group[-1] * span + span
            scores = lax.dot_general(
                held[step, 0, pair * span : end, :],
                held[step, 1, :end, :],
                (((1,), (1,)), ((), ())),
                preferred_element_type=jnp.float32,
            )
            for slot in group:
                count = (slot + 1) * span
                at = (slot - pair) * span
                ids = lax.broadcasted_iota(jnp.int32, (1, count), 1)
                valid = ids >= (slot - windows_ref[slot] + 1) * span
                masked = jnp.where(valid, scores[at : at + span, :count], -1e30)
                top = jnp.max(masked, axis=-1, keepdims=True)
                soft = jnp.exp2(masked - top)
                total = jnp.sum(soft, axis=-1, keepdims=True)
                summed = jnp.dot(
                    soft.astype(jnp.bfloat16),
                    held[step, 2, :count, :],
                    preferred_element_type=jnp.float32,
                )
                results[slot] = (summed / total).astype(jnp.bfloat16)
            for slot in group:

                @pl.when(slot_me != slot)
                def _(slot=slot):
                    give(step, slot, slot_me).start()

                @pl.when(slot_me == slot)
                def _():
                    settle.start()

        settle.wait()
        for slot in range(slots):

            @pl.when(slot_me != slot)
            def _(slot=slot):
                give(step, slot, slot).wait_recv()

        def relay_part(c):
            for s in range(2):
                part(c, s, 0).wait_recv()
                both = sent[c, block(near[1 - s]), half(s)].astype(jnp.float32) + got[
                    c, s, 0
                ].astype(jnp.float32)
                relay[c, s] = both.astype(jnp.bfloat16)
                part(c, s, 2).start()

        def finish(c):
            for s in range(2):
                at = slice(c * COLS + s * TILE, c * COLS + (s + 1) * TILE)
                part(c, s, 1).wait_recv()
                part(c, s, 2).wait_recv()
                total = (
                    sent[c, block(me), half(s)].astype(jnp.float32)
                    + got[c, s, 1].astype(jnp.float32)
                    + got[c, s, 2].astype(jnp.float32)
                )
                before = state[step, :, at].astype(jnp.float32)
                speed = (before + mod[2:3, at] * total).astype(jnp.bfloat16)
                speed_ref[step, :, at] = speed
                new_ref[:, at] = (before + factor * speed.astype(jnp.float32)).astype(
                    jnp.bfloat16
                )
            if step < STEPS - 1:

                @pl.when(slot_me > 0)
                def _():
                    hand_down(c, below).start()

        for c in range(chunks):
            if step == 0:
                fetch_outer(c).wait()
            for s in range(2):
                sent[c, :, s * TILE : (s + 1) * TILE] = jnp.dot(
                    attn[...],
                    outer[c, :, s * TILE : (s + 1) * TILE],
                    preferred_element_type=jnp.float32,
                ).astype(jnp.bfloat16)
                part(c, s, 0).start()
                part(c, s, 1).start()
            if c > 0:
                relay_part(c - 1)
            if c > 1:
                finish(c - 2)
        relay_part(last)
        if last > 0:
            finish(last - 1)
        finish(last)
        for c in range(chunks):
            for s in range(2):
                for kind in range(3):
                    part(c, s, kind).wait_send()
        for slot in range(slots):

            @pl.when(slot_me != slot)
            def _(slot=slot):
                push_v(step, slot, slot_me).wait_send()
                push_qk(step, slot, slot_me).wait_send()
                give(step, slot, slot_me).wait_send()

        if step < STEPS - 1:

            @pl.when(slot_me > 0)
            def _():
                for c in range(chunks):
                    hand_down(c, below).wait_send()

            @pl.when(slot_me < slots - 1)
            def _():
                for c in range(chunks):
                    hand_down(c, above).wait_recv()

            @pl.when(slot_me == slots - 1)
            def _():
                load_fresh.wait()


def fused(
    latent, fresh, levels, windows, plan, table, wq, wk, wv, wo, gq, gk, slots, heads
):
    rows, width = latent.shape
    span, features = rows * heads, wq.shape[1]
    chunks, heads_local = width // COLS, features // HD
    dma = pltpu.SemaphoreType.DMA
    bf16, f32 = jnp.bfloat16, jnp.float32
    return pl.pallas_call(
        functools.partial(fused_kernel, slots, heads),
        out_shape=(
            jax.ShapeDtypeStruct((STEPS, rows, width), bf16),
            jax.ShapeDtypeStruct((rows, width), bf16),
        ),
        in_specs=[SMEM] * 3 + [HBM] * 2 + [VMEM] + [HBM] * 4 + [VMEM] * 2,
        out_specs=(VMEM, VMEM),
        scratch_shapes=[
            pltpu.VMEM((STEPS, rows, width), bf16),
            pltpu.VMEM((3, width), f32),
            pltpu.VMEM((3, width, features), bf16),
            pltpu.VMEM((chunks, features, COLS), bf16),
            pltpu.VMEM((chunks, span, COLS), bf16),
            pltpu.VMEM((3, span, features), f32),
            pltpu.VMEM((2, 8, span), f32),
            pltpu.VMEM((heads - 1, 2, 8, span), f32),
            pltpu.VMEM((heads_local, 3, span, HD), bf16),
            pltpu.VMEM((STEPS, 3, slots * span, HD), bf16),
            pltpu.VMEM((slots, span, HD), bf16),
            pltpu.VMEM((span, features), bf16),
            pltpu.VMEM((chunks, span, COLS), bf16),
            pltpu.VMEM((chunks, 2, 3, rows, TILE), bf16),
            pltpu.VMEM((chunks, 2, rows, TILE), bf16),
            dma((2,)),
            dma((chunks, 3)),
            dma((chunks,)),
            dma((chunks, 2)),
            dma((chunks, 2)),
            dma((chunks, 2)),
            dma((chunks, 2)),
            dma((heads - 1,)),
            dma((heads - 1,)),
            dma((STEPS, slots)),
            dma((STEPS, slots)),
            dma((STEPS, slots)),
            dma((STEPS, slots)),
            dma((2,)),
            dma((STEPS, slots)),
            dma((STEPS, slots)),
            dma((chunks, 2, 3)),
            dma((chunks, 2, 3)),
            dma((chunks,)),
            dma((chunks,)),
        ],
        compiler_params=pltpu.CompilerParams(
            collective_id=0, has_side_effects=True, vmem_limit_bytes=58 * 2**20
        ),
        cost_estimate=pl.CostEstimate(
            flops=STEPS * 8 * span * width * features,
            bytes_accessed=8 * width * features,
            transcendentals=0,
        ),
        name="denoise",
    )(levels, windows, plan, latent, fresh, table, wq, wk, wv, wo, gq, gk)


def shifted(array, axis, by):
    length = lax.axis_size(axis)
    pairs = [(i, i + by) for i in range(length) if 0 <= i + by < length]
    return lax.ppermute(array, axis, pairs)


def embed(times, width):
    half = width // 2
    freq = jnp.exp(-math.log(10000.0) * jnp.arange(half, dtype=jnp.float32) / half)
    angle = times[:, None] * freq[None, :]
    return jnp.concatenate([jnp.cos(angle), jnp.sin(angle)], axis=-1)


def absorb(carry, keys, values, first_row, queries, lower, slot, span):
    top, total, summed = carry
    count = keys.shape[0]
    heads_local = keys.shape[1] // HD
    key_heads = keys.reshape(count, heads_local, HD)
    value_heads = values.reshape(count, heads_local, HD)
    scores = jnp.einsum(
        "qhd,khd->hqk", queries, key_heads, preferred_element_type=jnp.float32
    ) / math.sqrt(HD)
    span_ids = (first_row + jnp.arange(count, dtype=jnp.int32)) // span
    valid = ((span_ids >= lower) & (span_ids <= slot))[None, None, :]
    masked = jnp.where(valid, scores, -1e30)
    new_top = jnp.maximum(top, jnp.max(masked, axis=-1))
    weights = jnp.where(valid, jnp.exp(scores - new_top[:, :, None]), 0.0)
    fade = jnp.exp(top - new_top)
    total = total * fade + jnp.sum(weights, axis=-1)
    summed = summed * fade[:, :, None] + jnp.einsum(
        "hqk,khd->hqd",
        weights.astype(jnp.bfloat16),
        value_heads,
        preferred_element_type=jnp.float32,
    )
    return (new_top, total, summed)


def on_device(
    latent,
    fresh,
    levels,
    windows,
    plan,
    mod_table,
    w_query,
    w_key,
    w_value,
    w_out,
    query_gain,
    key_gain,
):
    queue_count = lax.axis_size("queue")
    head_count = lax.axis_size("head")
    slot = lax.axis_index("queue")
    rows = latent.shape[0]
    span = rows * head_count
    features = w_query.shape[1]
    heads_local = features // HD
    fits = latent.shape[1] % COLS == 0 and features % TILE == 0 and COLS == 2 * TILE
    if queue_count == heads_local and head_count == 4 and span == HD and fits:
        return fused(
            latent,
            fresh,
            levels,
            windows,
            plan,
            mod_table,
            w_query,
            w_key,
            w_value,
            w_out,
            query_gain[None],
            key_gain[None],
            queue_count,
            head_count,
        )
    table_hits = levels[:, None] == jnp.arange(plan.shape[0], dtype=jnp.int32)[None, :]
    t_all = jnp.sum(jnp.where(table_hits, plan[None, :], 0), axis=1).astype(jnp.float32)
    t_from = t_all[slot]
    t_to = jnp.where(slot > 0, t_all[jnp.maximum(slot - 1, 0)], 0.0)
    step_size = (t_to - t_from) / 1000.0
    lower = jnp.maximum(0, slot - windows[slot] + 1)
    emb = embed(t_from[None], latent.shape[1])[0]
    shift = mod_table[0] + emb
    scale = mod_table[1] + emb
    gate = mod_table[2] + emb
    state = latent
    speeds = []
    new = latent
    for step in range(STEPS):
        x = state.astype(jnp.float32)
        mean = jnp.mean(x, axis=-1, keepdims=True)
        var = jnp.mean((x - mean) ** 2, axis=-1, keepdims=True)
        normed = ((x - mean) * lax.rsqrt(var + 1e-06) * (1.0 + scale) + shift).astype(jnp.bfloat16)
        piece = lax.all_gather(normed, "head", axis=0, tiled=True)
        projected = jnp.concatenate(
            [
                jnp.dot(piece, w_query, preferred_element_type=jnp.float32),
                jnp.dot(piece, w_key, preferred_element_type=jnp.float32),
                jnp.dot(piece, w_value, preferred_element_type=jnp.float32),
            ],
            axis=-1,
        )
        q = projected[:, :features]
        k = projected[:, features : 2 * features]
        values = projected[:, 2 * features :].astype(jnp.bfloat16)
        query_sq, key_sq = lax.psum((jnp.sum(q * q, axis=-1), jnp.sum(k * k, axis=-1)), "head")
        every = features * head_count
        queries = (q * lax.rsqrt(query_sq / every + 1e-06)[:, None] * query_gain).astype(
            jnp.bfloat16
        )
        keys = (k * lax.rsqrt(key_sq / every + 1e-06)[:, None] * key_gain).astype(jnp.bfloat16)
        query_heads = queries.reshape(span, heads_local, HD)
        start_carry = (
            jnp.full((heads_local, span), -1e30, jnp.float32),
            jnp.zeros((heads_local, span), jnp.float32),
            jnp.zeros((heads_local, span, HD), jnp.float32),
        )
        inner = start_carry
        piece_keys = lax.all_gather(keys, "queue", axis=0, tiled=True)
        piece_values = lax.all_gather(values, "queue", axis=0, tiled=True)
        count = piece_keys.shape[0]
        blocks = count // span

        def one_block(running, block):
            block_keys, block_values, block_index = block
            return (
                absorb(
                    running,
                    block_keys,
                    block_values,
                    block_index * span,
                    query_heads,
                    lower,
                    slot,
                    span,
                ),
                None,
            )

        inner, unused = lax.scan(
            one_block,
            inner,
            (
                piece_keys.reshape(blocks, span, features),
                piece_values.reshape(blocks, span, features),
                jnp.arange(blocks, dtype=jnp.int32),
            ),
        )
        top, total, summed = inner
        attn = (
            jnp.transpose(summed / total[:, :, None], (1, 0, 2))
            .reshape(span, features)
            .astype(jnp.bfloat16)
        )
        mixed = lax.psum_scatter(
            jnp.dot(attn, w_out, preferred_element_type=jnp.float32).astype(jnp.bfloat16),
            "head",
            scatter_dimension=0,
            tiled=True,
        ).astype(jnp.float32)
        speed = (x + gate * mixed).astype(jnp.bfloat16)
        speeds.append(speed)
        new = (x + step_size * speed.astype(jnp.float32)).astype(jnp.bfloat16)
        if step < STEPS - 1:
            moved = shifted(new, "queue", -1)
            state = jnp.where(slot == queue_count - 1, fresh, moved)
    return (jnp.stack(speeds), new)


def solution(mesh):
    return jax.shard_map(
        on_device,
        mesh=mesh,
        in_specs=(
            P(("queue", "head"), None),
            P("head", None),
            P(),
            P(),
            P(),
            P(),
            P(None, "head"),
            P(None, "head"),
            P(None, "head"),
            P("head", None),
            P("head"),
            P("head"),
        ),
        out_specs=(P(None, ("queue", "head"), None), P(("queue", "head"), None)),
        check_vma=False,
    )
```

```python
import functools
import math

import jax
import jax.numpy as jnp
from jax import lax
from jax.experimental import pallas as pl
from jax.experimental.pallas import tpu as pltpu
from jax.sharding import PartitionSpec as P

HD = 128
STEPS = 2
COLS = 1024
TILE = 512
AHEAD = 5
BEHIND = 3
MESH = pl.DeviceIdType.MESH
VMEM = pl.BlockSpec(memory_space=pltpu.VMEM)
SMEM = pl.BlockSpec(memory_space=pltpu.SMEM)
HBM = pl.BlockSpec(memory_space=pl.ANY)


def fused_kernel(
    slots,
    heads,
    levels_ref,
    windows_ref,
    plan_ref,
    latent_ref,
    fresh_ref,
    table_ref,
    wq_ref,
    wk_ref,
    wv_ref,
    wo_ref,
    gq_ref,
    gk_ref,
    speed_ref,
    last_ref,
    new_ref,
    state,
    mod,
    weights,
    outer,
    gathered,
    acc,
    sums,
    sums_in,
    qkv,
    held,
    results,
    attn,
    sent,
    got,
    relay,
    in_sem,
    w_sem,
    o_sem,
    own_send,
    own_recv,
    fwd_send,
    fwd_recv,
    sum_send,
    sum_recv,
    v_send,
    v_recv,
    qk_send,
    qk_recv,
    local_sem,
    back_send,
    back_recv,
    part_send,
    part_recv,
    shift_send,
    shift_recv,
):
    slot_me = lax.axis_index("queue")
    me = lax.axis_index("head")
    across = me + 1 - 2 * lax.rem(me, 2)
    along = lax.rem(me + 2, heads)
    near = (across, along)
    far = lax.rem(across + 2, heads)
    rows, width = state.shape[1:]
    chunks, part_rows = gathered.shape[1:3]
    span = 2 * part_rows
    few = rows // 2
    last = chunks - 1
    stages = 2 * chunks
    features = wq_ref.shape[1]
    heads_local = features // HD
    sources = (wq_ref, wk_ref, wv_ref)

    def block(owner):
        return pl.ds(pl.multiple_of(owner * few, few), few)

    def cols(c):
        return slice(c * COLS, (c + 1) * COLS)

    def half(s):
        return pl.ds(s * TILE, TILE)

    load = pltpu.make_async_copy(latent_ref, state.at[0], in_sem.at[0])
    load_fresh = pltpu.make_async_copy(fresh_ref, state.at[1], in_sem.at[1])
    load.start()

    def fetch(c, m):
        at = pl.ds(c * COLS, COLS)
        return pltpu.make_async_copy(
            sources[m].at[at, :], weights.at[m, at, :], w_sem.at[c, m]
        )

    def fetch_outer(c):
        return pltpu.make_async_copy(
            wo_ref.at[:, pl.ds(c * COLS, COLS)], outer.at[c], o_sem.at[c]
        )

    for c in range(chunks):
        for m in range(3):
            fetch(c, m).start()
    for c in range(chunks):
        fetch_outer(c).start()

    @pl.when(slot_me == slots - 1)
    def _():
        load_fresh.start()

    barrier = pltpu.get_barrier_semaphore()
    for d in range(1, heads):
        pl.semaphore_signal(
            barrier, inc=1, device_id={"head": lax.rem(me + d, heads)}, device_id_type=MESH
        )
    for d in range(1, slots):
        pl.semaphore_signal(
            barrier, inc=1, device_id={"queue": lax.rem(slot_me + d, slots)}, device_id_type=MESH
        )

    t_from = plan_ref[levels_ref[slot_me]].astype(jnp.float32)
    t_below = plan_ref[levels_ref[jnp.maximum(slot_me - 1, 0)]].astype(jnp.float32)
    t_to = jnp.where(slot_me > 0, t_below, 0.0)
    factor = (t_to - t_from) / 1000.0
    mid = width // 2
    index = lax.broadcasted_iota(jnp.int32, (1, mid), 1).astype(jnp.float32)
    angle = t_from * jnp.exp(-math.log(10000.0) * index / mid)
    for at, emb in ((slice(0, mid), jnp.cos(angle)), (slice(mid, width), jnp.sin(angle))):
        mod[0:1, at] = table_ref[0:1, at] + emb
        mod[1:2, at] = 1.0 + (table_ref[1:2, at] + emb)
        mod[2:3, at] = table_ref[2:3, at] + emb

    pl.semaphore_wait(barrier, heads - 1 + slots - 1)
    load.wait()

    def own(k, way, owner):
        piece = gathered.at[k // chunks, k % chunks, block(owner), :]
        return pltpu.make_async_remote_copy(
            src_ref=piece,
            dst_ref=piece,
            send_sem=own_send.at[k, way],
            recv_sem=own_recv.at[k, way],
            device_id={"head": near[way]},
            device_id_type=MESH,
        )

    def forward(k, s, owner):
        piece = gathered.at[k // chunks, k % chunks, block(owner), half(s)]
        return pltpu.make_async_remote_copy(
            src_ref=piece,
            dst_ref=piece,
            send_sem=fwd_send.at[k, s],
            recv_sem=fwd_recv.at[k, s],
            device_id={"head": near[1 - s]},
            device_id_type=MESH,
        )

    def share(h, d):
        return pltpu.make_async_remote_copy(
            src_ref=sums.at[h],
            dst_ref=sums_in.at[h, d - 1],
            send_sem=sum_send.at[h, d - 1],
            recv_sem=sum_recv.at[h, d - 1],
            device_id={"head": lax.rem(me + d, heads)},
            device_id_type=MESH,
        )

    def multiply(k, first, end):
        h, c = k // chunks, k % chunks

        def one(m, carry):
            product = jnp.dot(
                gathered[h, c],
                weights[m, c * COLS : (c + 1) * COLS, :],
                preferred_element_type=jnp.float32,
            )
            acc[h, m] = product if c == 0 else acc[h, m] + product
            return carry

        lax.fori_loop(first, end, one, 0)

    def here(h):
        return slice(h * part_rows, (h + 1) * part_rows)

    def send_values(step, h):
        totals = []
        for m in range(2):
            value = acc[h, m]
            totals.append(jnp.sum(value * value, axis=-1, keepdims=True))
        wide = jnp.broadcast_to(jnp.concatenate(totals, axis=0), (span, span))
        sums[h] = jnp.transpose(wide)[:8]
        for d in range(1, heads):
            share(h, d).start()
        multiply(h * chunks + last, 2, 3)
        for j in range(heads_local):
            qkv[j, 2, here(h)] = acc[h, 2, :, j * HD : (j + 1) * HD].astype(jnp.bfloat16)
        for d in range(1, slots):
            push_v(step, h, lax.rem(slot_me + slots - d, slots), slot_me).start()

    def send_keys(step, h):
        total = sums[h]
        for d in range(1, heads):
            share(h, d).wait_recv()
            total = total + sums_in[h, d - 1]
        norm = lax.rsqrt(total / (features * heads) + 1e-06)
        column = jnp.transpose(jnp.broadcast_to(norm[:1], (span, span)))
        for m, gain_ref in ((0, gq_ref), (1, gk_ref)):
            scale = column[here(m)]
            if m == 0:
                scale = scale * (1.0 / (math.log(2.0) * math.sqrt(HD)))
            for j in range(heads_local):
                at = slice(j * HD, (j + 1) * HD)
                qkv[j, m, here(h)] = (acc[h, m, :, at] * scale * gain_ref[:, at]).astype(
                    jnp.bfloat16
                )
        for d in range(1, slots):
            push_qk(step, h, lax.rem(slot_me + slots - d, slots), slot_me).start()

    def rows_of(slot):
        return pl.ds(pl.multiple_of(slot * span, span), span)

    def columns_of(head):
        return pl.ds(pl.multiple_of(head * HD, HD), HD)

    def some_rows(slot, h):
        return pl.ds(pl.multiple_of(slot * span + h * part_rows, part_rows), part_rows)

    def push_v(step, h, peer, owner):
        return pltpu.make_async_remote_copy(
            src_ref=qkv.at[peer, 2, pl.ds(h * part_rows, part_rows), :],
            dst_ref=held.at[step, 2, some_rows(owner, h), :],
            send_sem=v_send.at[step, h, peer],
            recv_sem=v_recv.at[step, h, owner],
            device_id={"queue": peer},
            device_id_type=MESH,
        )

    def push_qk(step, h, peer, owner):
        return pltpu.make_async_remote_copy(
            src_ref=qkv.at[peer, 0:2, pl.ds(h * part_rows, part_rows), :],
            dst_ref=held.at[step, 0:2, some_rows(owner, h), :],
            send_sem=qk_send.at[step, h, peer],
            recv_sem=qk_recv.at[step, h, owner],
            device_id={"queue": peer},
            device_id_type=MESH,
        )

    def give(step, peer, head):
        return pltpu.make_async_remote_copy(
            src_ref=results.at[peer],
            dst_ref=attn.at[:, columns_of(head)],
            send_sem=back_send.at[step, peer],
            recv_sem=back_recv.at[step, head],
            device_id={"queue": peer},
            device_id_type=MESH,
        )

    def part(c, s, kind):
        target = near[s] if kind < 2 else near[1 - s]
        if kind == 0:
            source = sent.at[c, :, block(far), half(s)]
        elif kind == 1:
            source = sent.at[c, :, block(near[s]), half(s)]
        else:
            source = relay.at[c, s]
        return pltpu.make_async_remote_copy(
            src_ref=source,
            dst_ref=got.at[c, s, kind],
            send_sem=part_send.at[c, s, kind],
            recv_sem=part_recv.at[c, s, kind],
            device_id={"head": target},
            device_id_type=MESH,
        )

    def hand_down(c, peer):
        at = pl.ds(c * COLS, COLS)
        return pltpu.make_async_remote_copy(
            src_ref=new_ref.at[:, at],
            dst_ref=state.at[1, :, at],
            send_sem=shift_send.at[c],
            recv_sem=shift_recv.at[c],
            device_id={"queue": peer},
            device_id_type=MESH,
        )

    above = lax.rem(slot_me + 1, slots)
    below = lax.rem(slot_me + slots - 1, slots)

    for step in range(STEPS):
        x = state[step].astype(jnp.float32)
        mean = jnp.mean(x, axis=-1, keepdims=True)
        var = jnp.mean((x - mean) ** 2, axis=-1, keepdims=True)
        inv = lax.rsqrt(var + 1e-06)
        for c in range(chunks):
            piece = state[step, :, cols(c)].astype(jnp.float32)
            normed = (piece - mean) * inv * mod[1:2, cols(c)] + mod[0:1, cols(c)]
            for h in range(2):
                gathered[h, c, block(me), :] = normed[h * few : (h + 1) * few].astype(
                    jnp.bfloat16
                )
            if c < AHEAD:
                own(c, 0, me).start()
                own(c, 1, me).start()
        for k in range(stages + BEHIND):
            if k < stages:
                own(k, 0, across).wait_recv()
                forward(k, 0, across).start()
                own(k, 1, along).wait_recv()
                forward(k, 1, along).start()
                if k + AHEAD < stages:
                    own(k + AHEAD, 0, me).start()
                    own(k + AHEAD, 1, me).start()
            at = k - BEHIND
            if at >= 0:
                forward(at, 0, far).wait_recv()
                forward(at, 1, far).wait_recv()
                if step == 0 and at < chunks:
                    for m in range(3):
                        fetch(at, m).wait()
                ends = at % chunks == last
                multiply(at, 0, 2 if ends else 3)
                if ends:
                    send_values(step, at // chunks)
                if at == chunks + 1:
                    send_keys(step, 0)
        send_keys(step, 1)
        keep = pltpu.make_async_copy(
            qkv.at[slot_me], held.at[step, :, rows_of(slot_me), :], local_sem.at[0]
        )
        keep.start()
        for h in range(2):
            for d in range(1, heads):
                share(h, d).wait_send()
        for k in range(stages):
            for s in range(2):
                own(k, s, me).wait_send()
                forward(k, s, near[s]).wait_send()
        keep.wait()

        settle = pltpu.make_async_copy(
            results.at[slot_me], attn.at[:, columns_of(slot_me)], local_sem.at[1]
        )
        for pair in range(0, slots, 2):
            group = range(pair, min(pair + 2, slots))
            for slot in group:

                @pl.when(slot_me != slot)
                def _(slot=slot):
                    for h in range(2):
                        push_v(step, h, slot, slot).wait_recv()
                        push_qk(step, h, slot, slot).wait_recv()

            end = group[-1] * span + span
            scores = lax.dot_general(
                held[step, 0, pair * span : end, :],
                held[step, 1, :end, :],
                (((1,), (1,)), ((), ())),
                preferred_element_type=jnp.float32,
            )
            for slot in group:
                count = (slot + 1) * span
                at = (slot - pair) * span
                ids = lax.broadcasted_iota(jnp.int32, (1, count), 1)
                valid = ids >= (slot - windows_ref[slot] + 1) * span
                masked = jnp.where(valid, scores[at : at + span, :count], -1e30)
                top = jnp.max(masked, axis=-1, keepdims=True)
                soft = jnp.exp2(masked - top)
                total = jnp.sum(soft, axis=-1, keepdims=True)
                summed = jnp.dot(
                    soft.astype(jnp.bfloat16),
                    held[step, 2, :count, :],
                    preferred_element_type=jnp.float32,
                )
                results[slot] = (summed / total).astype(jnp.bfloat16)
            for slot in group:

                @pl.when(slot_me != slot)
                def _(slot=slot):
                    give(step, slot, slot_me).start()

                @pl.when(slot_me == slot)
                def _():
                    settle.start()

        settle.wait()
        for slot in range(slots):

            @pl.when(slot_me != slot)
            def _(slot=slot):
                give(step, slot, slot).wait_recv()

        def relay_part(c):
            for s in range(2):
                part(c, s, 0).wait_recv()
                both = sent[c, :, block(near[1 - s]), half(s)].astype(jnp.float32) + got[
                    c, s, 0
                ].astype(jnp.float32)
                relay[c, s] = both.astype(jnp.bfloat16)
                part(c, s, 2).start()

        def finish(c):
            for s in range(2):
                at = slice(c * COLS + s * TILE, c * COLS + (s + 1) * TILE)
                part(c, s, 1).wait_recv()
                part(c, s, 2).wait_recv()
                total = (
                    sent[c, :, block(me), half(s)].astype(jnp.float32)
                    + got[c, s, 1].astype(jnp.float32)
                    + got[c, s, 2].astype(jnp.float32)
                )
                total = total.reshape(rows, TILE)
                before = state[step, :, at].astype(jnp.float32)
                speed = (before + mod[2:3, at] * total).astype(jnp.bfloat16)
                (last_ref if step == STEPS - 1 else speed_ref)[:, at] = speed
                new_ref[:, at] = (before + factor * speed.astype(jnp.float32)).astype(
                    jnp.bfloat16
                )
            if step < STEPS - 1:

                @pl.when(slot_me > 0)
                def _():
                    hand_down(c, below).start()

        for c in range(chunks):
            if step == 0:
                fetch_outer(c).wait()
            for s in range(2):
                product = jnp.dot(
                    attn[...],
                    outer[c, :, s * TILE : (s + 1) * TILE],
                    preferred_element_type=jnp.float32,
                ).astype(jnp.bfloat16)
                for h in range(2):
                    sent[c, h, :, s * TILE : (s + 1) * TILE] = product[here(h)]
                part(c, s, 0).start()
                part(c, s, 1).start()
            if c > 0:
                relay_part(c - 1)
            if c > 1:
                finish(c - 2)
        relay_part(last)
        if last > 0:
            finish(last - 1)
        finish(last)
        for c in range(chunks):
            for s in range(2):
                for kind in range(3):
                    part(c, s, kind).wait_send()
        for slot in range(slots):

            @pl.when(slot_me != slot)
            def _(slot=slot):
                for h in range(2):
                    push_v(step, h, slot, slot_me).wait_send()
                    push_qk(step, h, slot, slot_me).wait_send()
                give(step, slot, slot_me).wait_send()

        if step < STEPS - 1:

            @pl.when(slot_me > 0)
            def _():
                for c in range(chunks):
                    hand_down(c, below).wait_send()

            @pl.when(slot_me < slots - 1)
            def _():
                for c in range(chunks):
                    hand_down(c, above).wait_recv()

            @pl.when(slot_me == slots - 1)
            def _():
                load_fresh.wait()


def fused(
    latent, fresh, levels, windows, plan, table, wq, wk, wv, wo, gq, gk, slots, heads
):
    rows, width = latent.shape
    span, features = rows * heads, wq.shape[1]
    chunks, heads_local = width // COLS, features // HD
    dma = pltpu.SemaphoreType.DMA
    bf16, f32 = jnp.bfloat16, jnp.float32
    return pl.pallas_call(
        functools.partial(fused_kernel, slots, heads),
        out_shape=(
            jax.ShapeDtypeStruct((rows, width), bf16),
            jax.ShapeDtypeStruct((rows, width), bf16),
            jax.ShapeDtypeStruct((rows, width), bf16),
        ),
        in_specs=[SMEM] * 3 + [HBM] * 2 + [VMEM] + [HBM] * 4 + [VMEM] * 2,
        out_specs=(VMEM, VMEM, VMEM),
        scratch_shapes=[
            pltpu.VMEM((STEPS, rows, width), bf16),
            pltpu.VMEM((3, width), f32),
            pltpu.VMEM((3, width, features), bf16),
            pltpu.VMEM((chunks, features, COLS), bf16),
            pltpu.VMEM((2, chunks, span // 2, COLS), bf16),
            pltpu.VMEM((2, 3, span // 2, features), f32),
            pltpu.VMEM((2, 8, span), f32),
            pltpu.VMEM((2, heads - 1, 8, span), f32),
            pltpu.VMEM((heads_local, 3, span, HD), bf16),
            pltpu.VMEM((STEPS, 3, slots * span, HD), bf16),
            pltpu.VMEM((slots, span, HD), bf16),
            pltpu.VMEM((span, features), bf16),
            pltpu.VMEM((chunks, 2, span // 2, COLS), bf16),
            pltpu.VMEM((chunks, 2, 3, 2, rows // 2, TILE), bf16),
            pltpu.VMEM((chunks, 2, 2, rows // 2, TILE), bf16),
            dma((2,)),
            dma((chunks, 3)),
            dma((chunks,)),
            dma((2 * chunks, 2)),
            dma((2 * chunks, 2)),
            dma((2 * chunks, 2)),
            dma((2 * chunks, 2)),
            dma((2, heads - 1)),
            dma((2, heads - 1)),
            dma((STEPS, 2, slots)),
            dma((STEPS, 2, slots)),
            dma((STEPS, 2, slots)),
            dma((STEPS, 2, slots)),
            dma((2,)),
            dma((STEPS, slots)),
            dma((STEPS, slots)),
            dma((chunks, 2, 3)),
            dma((chunks, 2, 3)),
            dma((chunks,)),
            dma((chunks,)),
        ],
        compiler_params=pltpu.CompilerParams(
            collective_id=0, has_side_effects=True, vmem_limit_bytes=54 * 2**20
        ),
        cost_estimate=pl.CostEstimate(
            flops=STEPS * 8 * span * width * features,
            bytes_accessed=8 * width * features,
            transcendentals=0,
        ),
        name="denoise",
    )(levels, windows, plan, latent, fresh, table, wq, wk, wv, wo, gq, gk)


def shifted(array, axis, by):
    length = lax.axis_size(axis)
    pairs = [(i, i + by) for i in range(length) if 0 <= i + by < length]
    return lax.ppermute(array, axis, pairs)


def embed(times, width):
    half = width // 2
    freq = jnp.exp(-math.log(10000.0) * jnp.arange(half, dtype=jnp.float32) / half)
    angle = times[:, None] * freq[None, :]
    return jnp.concatenate([jnp.cos(angle), jnp.sin(angle)], axis=-1)


def absorb(carry, keys, values, first_row, queries, lower, slot, span):
    top, total, summed = carry
    count = keys.shape[0]
    heads_local = keys.shape[1] // HD
    key_heads = keys.reshape(count, heads_local, HD)
    value_heads = values.reshape(count, heads_local, HD)
    scores = jnp.einsum(
        "qhd,khd->hqk", queries, key_heads, preferred_element_type=jnp.float32
    ) / math.sqrt(HD)
    span_ids = (first_row + jnp.arange(count, dtype=jnp.int32)) // span
    valid = ((span_ids >= lower) & (span_ids <= slot))[None, None, :]
    masked = jnp.where(valid, scores, -1e30)
    new_top = jnp.maximum(top, jnp.max(masked, axis=-1))
    weights = jnp.where(valid, jnp.exp(scores - new_top[:, :, None]), 0.0)
    fade = jnp.exp(top - new_top)
    total = total * fade + jnp.sum(weights, axis=-1)
    summed = summed * fade[:, :, None] + jnp.einsum(
        "hqk,khd->hqd",
        weights.astype(jnp.bfloat16),
        value_heads,
        preferred_element_type=jnp.float32,
    )
    return (new_top, total, summed)


def on_device(
    latent,
    fresh,
    levels,
    windows,
    plan,
    mod_table,
    w_query,
    w_key,
    w_value,
    w_out,
    query_gain,
    key_gain,
):
    queue_count = lax.axis_size("queue")
    head_count = lax.axis_size("head")
    slot = lax.axis_index("queue")
    rows = latent.shape[0]
    span = rows * head_count
    features = w_query.shape[1]
    heads_local = features // HD
    fits = latent.shape[1] % COLS == 0 and features % TILE == 0 and COLS == 2 * TILE
    if queue_count == heads_local and head_count == 4 and span == HD and rows % 32 == 0 and fits:
        first, second, new = fused(
            latent,
            fresh,
            levels,
            windows,
            plan,
            mod_table,
            w_query,
            w_key,
            w_value,
            w_out,
            query_gain[None],
            key_gain[None],
            queue_count,
            head_count,
        )
        return (jnp.stack([first, second]), new)
    table_hits = levels[:, None] == jnp.arange(plan.shape[0], dtype=jnp.int32)[None, :]
    t_all = jnp.sum(jnp.where(table_hits, plan[None, :], 0), axis=1).astype(jnp.float32)
    t_from = t_all[slot]
    t_to = jnp.where(slot > 0, t_all[jnp.maximum(slot - 1, 0)], 0.0)
    step_size = (t_to - t_from) / 1000.0
    lower = jnp.maximum(0, slot - windows[slot] + 1)
    emb = embed(t_from[None], latent.shape[1])[0]
    shift = mod_table[0] + emb
    scale = mod_table[1] + emb
    gate = mod_table[2] + emb
    state = latent
    speeds = []
    new = latent
    for step in range(STEPS):
        x = state.astype(jnp.float32)
        mean = jnp.mean(x, axis=-1, keepdims=True)
        var = jnp.mean((x - mean) ** 2, axis=-1, keepdims=True)
        normed = ((x - mean) * lax.rsqrt(var + 1e-06) * (1.0 + scale) + shift).astype(jnp.bfloat16)
        piece = lax.all_gather(normed, "head", axis=0, tiled=True)
        projected = jnp.concatenate(
            [
                jnp.dot(piece, w_query, preferred_element_type=jnp.float32),
                jnp.dot(piece, w_key, preferred_element_type=jnp.float32),
                jnp.dot(piece, w_value, preferred_element_type=jnp.float32),
            ],
            axis=-1,
        )
        q = projected[:, :features]
        k = projected[:, features : 2 * features]
        values = projected[:, 2 * features :].astype(jnp.bfloat16)
        query_sq, key_sq = lax.psum((jnp.sum(q * q, axis=-1), jnp.sum(k * k, axis=-1)), "head")
        every = features * head_count
        queries = (q * lax.rsqrt(query_sq / every + 1e-06)[:, None] * query_gain).astype(
            jnp.bfloat16
        )
        keys = (k * lax.rsqrt(key_sq / every + 1e-06)[:, None] * key_gain).astype(jnp.bfloat16)
        query_heads = queries.reshape(span, heads_local, HD)
        start_carry = (
            jnp.full((heads_local, span), -1e30, jnp.float32),
            jnp.zeros((heads_local, span), jnp.float32),
            jnp.zeros((heads_local, span, HD), jnp.float32),
        )
        inner = start_carry
        piece_keys = lax.all_gather(keys, "queue", axis=0, tiled=True)
        piece_values = lax.all_gather(values, "queue", axis=0, tiled=True)
        count = piece_keys.shape[0]
        blocks = count // span

        def one_block(running, block):
            block_keys, block_values, block_index = block
            return (
                absorb(
                    running,
                    block_keys,
                    block_values,
                    block_index * span,
                    query_heads,
                    lower,
                    slot,
                    span,
                ),
                None,
            )

        inner, unused = lax.scan(
            one_block,
            inner,
            (
                piece_keys.reshape(blocks, span, features),
                piece_values.reshape(blocks, span, features),
                jnp.arange(blocks, dtype=jnp.int32),
            ),
        )
        top, total, summed = inner
        attn = (
            jnp.transpose(summed / total[:, :, None], (1, 0, 2))
            .reshape(span, features)
            .astype(jnp.bfloat16)
        )
        mixed = lax.psum_scatter(
            jnp.dot(attn, w_out, preferred_element_type=jnp.float32).astype(jnp.bfloat16),
            "head",
            scatter_dimension=0,
            tiled=True,
        ).astype(jnp.float32)
        speed = (x + gate * mixed).astype(jnp.bfloat16)
        speeds.append(speed)
        new = (x + step_size * speed.astype(jnp.float32)).astype(jnp.bfloat16)
        if step < STEPS - 1:
            moved = shifted(new, "queue", -1)
            state = jnp.where(slot == queue_count - 1, fresh, moved)
    return (jnp.stack(speeds), new)


def solution(mesh):
    return jax.shard_map(
        on_device,
        mesh=mesh,
        in_specs=(
            P(("queue", "head"), None),
            P("head", None),
            P(),
            P(),
            P(),
            P(),
            P(None, "head"),
            P(None, "head"),
            P(None, "head"),
            P("head", None),
            P("head"),
            P("head"),
        ),
        out_specs=(P(None, ("queue", "head"), None), P(("queue", "head"), None)),
        check_vma=False,
    )
```

```python
import functools
import math

import jax
import jax.numpy as jnp
from jax import lax
from jax.experimental import pallas as pl
from jax.experimental.pallas import tpu as pltpu
from jax.sharding import PartitionSpec as P

HD = 128
STEPS = 2
COLS = 1024
TILE = 512
BEHIND = 3
MESH = pl.DeviceIdType.MESH
VMEM = pl.BlockSpec(memory_space=pltpu.VMEM)
SMEM = pl.BlockSpec(memory_space=pltpu.SMEM)
HBM = pl.BlockSpec(memory_space=pl.ANY)


def each(count, body):
    def one(i, carry):
        body(i)
        return carry

    lax.fori_loop(0, count, one, 0)


def fused_kernel(
    slots,
    heads,
    levels_ref,
    windows_ref,
    plan_ref,
    latent_ref,
    fresh_ref,
    table_ref,
    wq_ref,
    wk_ref,
    wv_ref,
    wo_ref,
    gq_ref,
    gk_ref,
    speed_ref,
    new_ref,
    state,
    mod,
    weights,
    outer,
    gathered,
    acc,
    sums,
    sums_in,
    qkv,
    held,
    results,
    attn,
    sent,
    got,
    relay,
    in_sem,
    w_sem,
    o_sem,
    own_send,
    own_recv,
    fwd_send,
    fwd_recv,
    sum_send,
    sum_recv,
    v_send,
    v_recv,
    qk_send,
    qk_recv,
    local_sem,
    back_send,
    back_recv,
    part_send,
    part_recv,
    shift_send,
    shift_recv,
):
    slot_me = lax.axis_index("queue")
    me = lax.axis_index("head")
    across = me + 1 - 2 * lax.rem(me, 2)
    along = lax.rem(me + 2, heads)
    near = (across, along)
    far = lax.rem(across + 2, heads)
    rows, width = state.shape[1:]
    chunks, part_rows = gathered.shape[1:3]
    span = 2 * part_rows
    few = rows // 2
    last = chunks - 1
    stages = 2 * chunks
    features = wq_ref.shape[1]
    heads_local = features // HD
    sources = (wq_ref, wk_ref, wv_ref)

    def block(owner):
        return pl.ds(pl.multiple_of(owner * few, few), few)

    def cols(c):
        return pl.ds(pl.multiple_of(c * COLS, COLS), COLS)

    def half(s):
        return pl.ds(s * TILE, TILE)

    load = pltpu.make_async_copy(latent_ref, state.at[0], in_sem.at[0])
    load_fresh = pltpu.make_async_copy(fresh_ref, state.at[1], in_sem.at[1])
    load.start()

    def fetch(c, m):
        at = cols(c)
        return pltpu.make_async_copy(
            sources[m].at[at, :], weights.at[m, at, :], w_sem.at[c, m]
        )

    def fetch_outer(c):
        return pltpu.make_async_copy(
            wo_ref.at[:, cols(c)], outer.at[c], o_sem.at[c]
        )

    @functools.partial(each, chunks)
    def _(c):
        for m in range(3):
            fetch(c, m).start()

    each(chunks, lambda c: fetch_outer(c).start())

    @pl.when(slot_me == slots - 1)
    def _():
        load_fresh.start()

    barrier = pltpu.get_barrier_semaphore()
    for d in range(1, heads):
        pl.semaphore_signal(
            barrier, inc=1, device_id={"head": lax.rem(me + d, heads)}, device_id_type=MESH
        )
    for d in range(1, slots):
        pl.semaphore_signal(
            barrier, inc=1, device_id={"queue": lax.rem(slot_me + d, slots)}, device_id_type=MESH
        )

    t_from = plan_ref[levels_ref[slot_me]].astype(jnp.float32)
    t_below = plan_ref[levels_ref[jnp.maximum(slot_me - 1, 0)]].astype(jnp.float32)
    t_to = jnp.where(slot_me > 0, t_below, 0.0)
    factor = (t_to - t_from) / 1000.0
    mid = width // 2
    index = lax.broadcasted_iota(jnp.int32, (1, mid), 1).astype(jnp.float32)
    angle = t_from * jnp.exp(-math.log(10000.0) * index / mid)
    for at, emb in ((slice(0, mid), jnp.cos(angle)), (slice(mid, width), jnp.sin(angle))):
        mod[0:1, at] = table_ref[0:1, at] + emb
        mod[1:2, at] = 1.0 + (table_ref[1:2, at] + emb)
        mod[2:3, at] = table_ref[2:3, at] + emb

    pl.semaphore_wait(barrier, heads - 1 + slots - 1)
    load.wait()

    def own(k, way, owner):
        piece = gathered.at[k // chunks, k % chunks, block(owner), :]
        return pltpu.make_async_remote_copy(
            src_ref=piece,
            dst_ref=piece,
            send_sem=own_send.at[k, way],
            recv_sem=own_recv.at[k, way],
            device_id={"head": near[way]},
            device_id_type=MESH,
        )

    def forward(k, s, owner):
        piece = gathered.at[k // chunks, k % chunks, block(owner), half(s)]
        return pltpu.make_async_remote_copy(
            src_ref=piece,
            dst_ref=piece,
            send_sem=fwd_send.at[k, s],
            recv_sem=fwd_recv.at[k, s],
            device_id={"head": near[1 - s]},
            device_id_type=MESH,
        )

    def share(h, d):
        return pltpu.make_async_remote_copy(
            src_ref=sums.at[h],
            dst_ref=sums_in.at[h, d - 1],
            send_sem=sum_send.at[h, d - 1],
            recv_sem=sum_recv.at[h, d - 1],
            device_id={"head": lax.rem(me + d, heads)},
            device_id_type=MESH,
        )

    def multiply(k):
        h, c = k // chunks, k % chunks

        @functools.partial(each, 3)
        def _(m):
            product = jnp.dot(
                gathered[h, c], weights[m, cols(c), :], preferred_element_type=jnp.float32
            )
            acc[h, m] = jnp.where(c == 0, product, acc[h, m] + product)

    def here(h):
        return pl.ds(pl.multiple_of(h * part_rows, part_rows), part_rows)

    def send_values(step, h):
        totals = []
        for m in range(2):
            value = acc[h, m]
            totals.append(jnp.sum(value * value, axis=-1, keepdims=True))
        wide = jnp.broadcast_to(jnp.concatenate(totals, axis=0), (span, span))
        sums[h] = jnp.transpose(wide)[:8]
        for d in range(1, heads):
            share(h, d).start()
        for j in range(heads_local):
            qkv[j, 2, here(h)] = acc[h, 2, :, j * HD : (j + 1) * HD].astype(jnp.bfloat16)

        @functools.partial(each, slots - 1)
        def _(d):
            push_v(step, h, lax.rem(slot_me + slots - 1 - d, slots), slot_me).start()

    def send_keys(step, h):
        total = sums[h]
        for d in range(1, heads):
            share(h, d).wait_recv()
            total = total + sums_in[h, d - 1]
        norm = lax.rsqrt(total / (features * heads) + 1e-06)
        column = jnp.transpose(jnp.broadcast_to(norm[:1], (span, span)))
        for m, gain_ref in ((0, gq_ref), (1, gk_ref)):
            scale = column[m * part_rows : (m + 1) * part_rows]
            if m == 0:
                scale = scale * (1.0 / (math.log(2.0) * math.sqrt(HD)))
            for j in range(heads_local):
                at = slice(j * HD, (j + 1) * HD)
                qkv[j, m, here(h)] = (acc[h, m, :, at] * scale * gain_ref[:, at]).astype(
                    jnp.bfloat16
                )

        @functools.partial(each, slots - 1)
        def _(d):
            push_qk(step, h, lax.rem(slot_me + slots - 1 - d, slots), slot_me).start()

    def rows_of(slot):
        return pl.ds(pl.multiple_of(slot * span, span), span)

    def columns_of(head):
        return pl.ds(pl.multiple_of(head * HD, HD), HD)

    def some_rows(slot, h):
        return pl.ds(pl.multiple_of(slot * span + h * part_rows, part_rows), part_rows)

    def push_v(step, h, peer, owner):
        return pltpu.make_async_remote_copy(
            src_ref=qkv.at[peer, 2, here(h), :],
            dst_ref=held.at[step, 2, some_rows(owner, h), :],
            send_sem=v_send.at[step, h, peer],
            recv_sem=v_recv.at[step, h, owner],
            device_id={"queue": peer},
            device_id_type=MESH,
        )

    def push_qk(step, h, peer, owner):
        return pltpu.make_async_remote_copy(
            src_ref=qkv.at[peer, 0:2, here(h), :],
            dst_ref=held.at[step, 0:2, some_rows(owner, h), :],
            send_sem=qk_send.at[step, h, peer],
            recv_sem=qk_recv.at[step, h, owner],
            device_id={"queue": peer},
            device_id_type=MESH,
        )

    def give(step, peer, head):
        return pltpu.make_async_remote_copy(
            src_ref=results.at[peer],
            dst_ref=attn.at[:, columns_of(head)],
            send_sem=back_send.at[step, peer],
            recv_sem=back_recv.at[step, head],
            device_id={"queue": peer},
            device_id_type=MESH,
        )

    def part(c, s, kind):
        target = near[s] if kind < 2 else near[1 - s]
        if kind == 0:
            source = sent.at[c, :, block(far), half(s)]
        elif kind == 1:
            source = sent.at[c, :, block(near[s]), half(s)]
        else:
            source = relay.at[c, s]
        return pltpu.make_async_remote_copy(
            src_ref=source,
            dst_ref=got.at[c, s, kind],
            send_sem=part_send.at[c, s, kind],
            recv_sem=part_recv.at[c, s, kind],
            device_id={"head": target},
            device_id_type=MESH,
        )

    def hand_down(c, peer):
        at = cols(c)
        return pltpu.make_async_remote_copy(
            src_ref=new_ref.at[:, at],
            dst_ref=state.at[1, :, at],
            send_sem=shift_send.at[c],
            recv_sem=shift_recv.at[c],
            device_id={"queue": peer},
            device_id_type=MESH,
        )

    above = lax.rem(slot_me + 1, slots)
    below = lax.rem(slot_me + slots - 1, slots)

    @functools.partial(each, STEPS)
    def _(step):
        x = state[step].astype(jnp.float32)
        mean = jnp.mean(x, axis=-1, keepdims=True)
        var = jnp.mean((x - mean) ** 2, axis=-1, keepdims=True)
        inv = lax.rsqrt(var + 1e-06)

        @functools.partial(each, chunks)
        def _(c):
            piece = state[step, :, cols(c)].astype(jnp.float32)
            normed = (piece - mean) * inv * mod[1:2, cols(c)] + mod[0:1, cols(c)]
            for h in range(2):
                gathered[h, c, block(me), :] = normed[h * few : (h + 1) * few].astype(
                    jnp.bfloat16
                )
            own(c, 0, me).start()
            own(c, 1, me).start()

        @functools.partial(each, stages + BEHIND)
        def _(k):
            @pl.when(k < stages)
            def _():
                own(k, 0, across).wait_recv()
                forward(k, 0, across).start()
                own(k, 1, along).wait_recv()
                forward(k, 1, along).start()

            @pl.when(k < chunks)
            def _():
                own(k + chunks, 0, me).start()
                own(k + chunks, 1, me).start()

            at = k - BEHIND

            @pl.when(at >= 0)
            def _():
                forward(at, 0, far).wait_recv()
                forward(at, 1, far).wait_recv()

                @pl.when((step == 0) & (at < chunks))
                def _():
                    for m in range(3):
                        fetch(at, m).wait()

                multiply(at)

                @pl.when(at % chunks == last)
                def _():
                    send_values(step, at // chunks)

                @pl.when((at == chunks + 1) | (at == stages - 1))
                def _():
                    send_keys(step, at // stages + (at + 1) // stages)

        keep = pltpu.make_async_copy(
            qkv.at[slot_me], held.at[step, :, rows_of(slot_me), :], local_sem.at[0]
        )
        keep.start()
        for h in range(2):
            for d in range(1, heads):
                share(h, d).wait_send()

        @functools.partial(each, stages)
        def _(k):
            for s in range(2):
                own(k, s, me).wait_send()
                forward(k, s, near[s]).wait_send()

        keep.wait()

        settle = pltpu.make_async_copy(
            results.at[slot_me], attn.at[:, columns_of(slot_me)], local_sem.at[1]
        )
        for pair in range(0, slots, 2):
            group = range(pair, min(pair + 2, slots))
            for slot in group:

                @pl.when(slot_me != slot)
                def _(slot=slot):
                    for h in range(2):
                        push_v(step, h, slot, slot).wait_recv()
                        push_qk(step, h, slot, slot).wait_recv()

            end = group[-1] * span + span
            scores = lax.dot_general(
                held[step, 0, pair * span : end, :],
                held[step, 1, :end, :],
                (((1,), (1,)), ((), ())),
                preferred_element_type=jnp.float32,
            )
            for slot in group:
                count = (slot + 1) * span
                at = (slot - pair) * span
                ids = lax.broadcasted_iota(jnp.int32, (1, count), 1)
                valid = ids >= (slot - windows_ref[slot] + 1) * span
                masked = jnp.where(valid, scores[at : at + span, :count], -1e30)
                top = jnp.max(masked, axis=-1, keepdims=True)
                soft = jnp.exp2(masked - top)
                total = jnp.sum(soft, axis=-1, keepdims=True)
                summed = jnp.dot(
                    soft.astype(jnp.bfloat16),
                    held[step, 2, :count, :],
                    preferred_element_type=jnp.float32,
                )
                results[slot] = (summed / total).astype(jnp.bfloat16)
            for slot in group:

                @pl.when(slot_me != slot)
                def _(slot=slot):
                    give(step, slot, slot_me).start()

                @pl.when(slot_me == slot)
                def _():
                    settle.start()

        settle.wait()

        @functools.partial(each, slots)
        def _(slot):
            @pl.when(slot_me != slot)
            def _():
                give(step, slot, slot).wait_recv()

        def relay_part(c):
            for s in range(2):
                part(c, s, 0).wait_recv()
                both = sent[c, :, block(near[1 - s]), half(s)].astype(jnp.float32) + got[
                    c, s, 0
                ].astype(jnp.float32)
                relay[c, s] = both.astype(jnp.bfloat16)
                part(c, s, 2).start()

        def finish(c):
            for s in range(2):
                at = pl.ds(pl.multiple_of(c * COLS + s * TILE, TILE), TILE)
                part(c, s, 1).wait_recv()
                part(c, s, 2).wait_recv()
                total = (
                    sent[c, :, block(me), half(s)].astype(jnp.float32)
                    + got[c, s, 1].astype(jnp.float32)
                    + got[c, s, 2].astype(jnp.float32)
                )
                total = total.reshape(rows, TILE)
                before = state[step, :, at].astype(jnp.float32)
                speed = (before + mod[2:3, at] * total).astype(jnp.bfloat16)
                speed_ref[step, :, at] = speed
                new_ref[:, at] = (before + factor * speed.astype(jnp.float32)).astype(
                    jnp.bfloat16
                )

            @pl.when((step < STEPS - 1) & (slot_me > 0))
            def _():
                hand_down(c, below).start()

        @functools.partial(each, chunks + 2)
        def _(c):
            @pl.when(c < chunks)
            def _():
                @pl.when(step == 0)
                def _():
                    fetch_outer(c).wait()

                for s in range(2):
                    product = jnp.dot(
                        attn[...],
                        outer[c, :, s * TILE : (s + 1) * TILE],
                        preferred_element_type=jnp.float32,
                    ).astype(jnp.bfloat16)
                    for h in range(2):
                        sent[c, h, :, s * TILE : (s + 1) * TILE] = product[
                            h * part_rows : (h + 1) * part_rows
                        ]
                    part(c, s, 0).start()
                    part(c, s, 1).start()

            @pl.when((c > 0) & (c <= chunks))
            def _():
                relay_part(c - 1)

            @pl.when(c > 1)
            def _():
                finish(c - 2)

        @functools.partial(each, chunks)
        def _(c):
            for s in range(2):
                for kind in range(3):
                    part(c, s, kind).wait_send()

        @functools.partial(each, slots)
        def _(slot):
            @pl.when(slot_me != slot)
            def _():
                for h in range(2):
                    push_v(step, h, slot, slot_me).wait_send()
                    push_qk(step, h, slot, slot_me).wait_send()
                give(step, slot, slot_me).wait_send()

        @pl.when(step < STEPS - 1)
        def _():
            @pl.when(slot_me > 0)
            def _():
                each(chunks, lambda c: hand_down(c, below).wait_send())

            @pl.when(slot_me < slots - 1)
            def _():
                each(chunks, lambda c: hand_down(c, above).wait_recv())

            @pl.when(slot_me == slots - 1)
            def _():
                load_fresh.wait()


def fused(
    latent, fresh, levels, windows, plan, table, wq, wk, wv, wo, gq, gk, slots, heads
):
    rows, width = latent.shape
    span, features = rows * heads, wq.shape[1]
    chunks, heads_local = width // COLS, features // HD
    dma = pltpu.SemaphoreType.DMA
    bf16, f32 = jnp.bfloat16, jnp.float32
    return pl.pallas_call(
        functools.partial(fused_kernel, slots, heads),
        out_shape=(
            jax.ShapeDtypeStruct((STEPS, rows, width), bf16),
            jax.ShapeDtypeStruct((rows, width), bf16),
        ),
        in_specs=[SMEM] * 3 + [HBM] * 2 + [VMEM] + [HBM] * 4 + [VMEM] * 2,
        out_specs=(VMEM, VMEM),
        scratch_shapes=[
            pltpu.VMEM((STEPS, rows, width), bf16),
            pltpu.VMEM((3, width), f32),
            pltpu.VMEM((3, width, features), bf16),
            pltpu.VMEM((chunks, features, COLS), bf16),
            pltpu.VMEM((2, chunks, span // 2, COLS), bf16),
            pltpu.VMEM((2, 3, span // 2, features), f32),
            pltpu.VMEM((2, 8, span), f32),
            pltpu.VMEM((2, heads - 1, 8, span), f32),
            pltpu.VMEM((heads_local, 3, span, HD), bf16),
            pltpu.VMEM((STEPS, 3, slots * span, HD), bf16),
            pltpu.VMEM((slots, span, HD), bf16),
            pltpu.VMEM((span, features), bf16),
            pltpu.VMEM((chunks, 2, span // 2, COLS), bf16),
            pltpu.VMEM((chunks, 2, 3, 2, rows // 2, TILE), bf16),
            pltpu.VMEM((chunks, 2, 2, rows // 2, TILE), bf16),
            dma((2,)),
            dma((chunks, 3)),
            dma((chunks,)),
            dma((2 * chunks, 2)),
            dma((2 * chunks, 2)),
            dma((2 * chunks, 2)),
            dma((2 * chunks, 2)),
            dma((2, heads - 1)),
            dma((2, heads - 1)),
            dma((STEPS, 2, slots)),
            dma((STEPS, 2, slots)),
            dma((STEPS, 2, slots)),
            dma((STEPS, 2, slots)),
            dma((2,)),
            dma((STEPS, slots)),
            dma((STEPS, slots)),
            dma((chunks, 2, 3)),
            dma((chunks, 2, 3)),
            dma((chunks,)),
            dma((chunks,)),
        ],
        compiler_params=pltpu.CompilerParams(
            collective_id=0, has_side_effects=True, vmem_limit_bytes=54 * 2**20
        ),
        cost_estimate=pl.CostEstimate(
            flops=STEPS * 8 * span * width * features,
            bytes_accessed=8 * width * features,
            transcendentals=0,
        ),
        name="denoise",
    )(levels, windows, plan, latent, fresh, table, wq, wk, wv, wo, gq, gk)


def shifted(array, axis, by):
    length = lax.axis_size(axis)
    pairs = [(i, i + by) for i in range(length) if 0 <= i + by < length]
    return lax.ppermute(array, axis, pairs)


def embed(times, width):
    half = width // 2
    freq = jnp.exp(-math.log(10000.0) * jnp.arange(half, dtype=jnp.float32) / half)
    angle = times[:, None] * freq[None, :]
    return jnp.concatenate([jnp.cos(angle), jnp.sin(angle)], axis=-1)


def absorb(carry, keys, values, first_row, queries, lower, slot, span):
    top, total, summed = carry
    count = keys.shape[0]
    heads_local = keys.shape[1] // HD
    key_heads = keys.reshape(count, heads_local, HD)
    value_heads = values.reshape(count, heads_local, HD)
    scores = jnp.einsum(
        "qhd,khd->hqk", queries, key_heads, preferred_element_type=jnp.float32
    ) / math.sqrt(HD)
    span_ids = (first_row + jnp.arange(count, dtype=jnp.int32)) // span
    valid = ((span_ids >= lower) & (span_ids <= slot))[None, None, :]
    masked = jnp.where(valid, scores, -1e30)
    new_top = jnp.maximum(top, jnp.max(masked, axis=-1))
    weights = jnp.where(valid, jnp.exp(scores - new_top[:, :, None]), 0.0)
    fade = jnp.exp(top - new_top)
    total = total * fade + jnp.sum(weights, axis=-1)
    summed = summed * fade[:, :, None] + jnp.einsum(
        "hqk,khd->hqd",
        weights.astype(jnp.bfloat16),
        value_heads,
        preferred_element_type=jnp.float32,
    )
    return (new_top, total, summed)


def on_device(
    latent,
    fresh,
    levels,
    windows,
    plan,
    mod_table,
    w_query,
    w_key,
    w_value,
    w_out,
    query_gain,
    key_gain,
):
    queue_count = lax.axis_size("queue")
    head_count = lax.axis_size("head")
    slot = lax.axis_index("queue")
    rows = latent.shape[0]
    span = rows * head_count
    features = w_query.shape[1]
    heads_local = features // HD
    fits = latent.shape[1] % COLS == 0 and features % TILE == 0 and COLS == 2 * TILE
    if queue_count == heads_local and head_count == 4 and span == HD and rows % 32 == 0 and fits:
        return fused(
            latent,
            fresh,
            levels,
            windows,
            plan,
            mod_table,
            w_query,
            w_key,
            w_value,
            w_out,
            query_gain[None],
            key_gain[None],
            queue_count,
            head_count,
        )
    table_hits = levels[:, None] == jnp.arange(plan.shape[0], dtype=jnp.int32)[None, :]
    t_all = jnp.sum(jnp.where(table_hits, plan[None, :], 0), axis=1).astype(jnp.float32)
    t_from = t_all[slot]
    t_to = jnp.where(slot > 0, t_all[jnp.maximum(slot - 1, 0)], 0.0)
    step_size = (t_to - t_from) / 1000.0
    lower = jnp.maximum(0, slot - windows[slot] + 1)
    emb = embed(t_from[None], latent.shape[1])[0]
    shift = mod_table[0] + emb
    scale = mod_table[1] + emb
    gate = mod_table[2] + emb
    state = latent
    speeds = []
    new = latent
    for step in range(STEPS):
        x = state.astype(jnp.float32)
        mean = jnp.mean(x, axis=-1, keepdims=True)
        var = jnp.mean((x - mean) ** 2, axis=-1, keepdims=True)
        normed = ((x - mean) * lax.rsqrt(var + 1e-06) * (1.0 + scale) + shift).astype(jnp.bfloat16)
        piece = lax.all_gather(normed, "head", axis=0, tiled=True)
        projected = jnp.concatenate(
            [
                jnp.dot(piece, w_query, preferred_element_type=jnp.float32),
                jnp.dot(piece, w_key, preferred_element_type=jnp.float32),
                jnp.dot(piece, w_value, preferred_element_type=jnp.float32),
            ],
            axis=-1,
        )
        q = projected[:, :features]
        k = projected[:, features : 2 * features]
        values = projected[:, 2 * features :].astype(jnp.bfloat16)
        query_sq, key_sq = lax.psum((jnp.sum(q * q, axis=-1), jnp.sum(k * k, axis=-1)), "head")
        every = features * head_count
        queries = (q * lax.rsqrt(query_sq / every + 1e-06)[:, None] * query_gain).astype(
            jnp.bfloat16
        )
        keys = (k * lax.rsqrt(key_sq / every + 1e-06)[:, None] * key_gain).astype(jnp.bfloat16)
        query_heads = queries.reshape(span, heads_local, HD)
        start_carry = (
            jnp.full((heads_local, span), -1e30, jnp.float32),
            jnp.zeros((heads_local, span), jnp.float32),
            jnp.zeros((heads_local, span, HD), jnp.float32),
        )
        inner = start_carry
        piece_keys = lax.all_gather(keys, "queue", axis=0, tiled=True)
        piece_values = lax.all_gather(values, "queue", axis=0, tiled=True)
        count = piece_keys.shape[0]
        blocks = count // span

        def one_block(running, block):
            block_keys, block_values, block_index = block
            return (
                absorb(
                    running,
                    block_keys,
                    block_values,
                    block_index * span,
                    query_heads,
                    lower,
                    slot,
                    span,
                ),
                None,
            )

        inner, unused = lax.scan(
            one_block,
            inner,
            (
                piece_keys.reshape(blocks, span, features),
                piece_values.reshape(blocks, span, features),
                jnp.arange(blocks, dtype=jnp.int32),
            ),
        )
        top, total, summed = inner
        attn = (
            jnp.transpose(summed / total[:, :, None], (1, 0, 2))
            .reshape(span, features)
            .astype(jnp.bfloat16)
        )
        mixed = lax.psum_scatter(
            jnp.dot(attn, w_out, preferred_element_type=jnp.float32).astype(jnp.bfloat16),
            "head",
            scatter_dimension=0,
            tiled=True,
        ).astype(jnp.float32)
        speed = (x + gate * mixed).astype(jnp.bfloat16)
        speeds.append(speed)
        new = (x + step_size * speed.astype(jnp.float32)).astype(jnp.bfloat16)
        if step < STEPS - 1:
            moved = shifted(new, "queue", -1)
            state = jnp.where(slot == queue_count - 1, fresh, moved)
    return (jnp.stack(speeds), new)


def solution(mesh):
    return jax.shard_map(
        on_device,
        mesh=mesh,
        in_specs=(
            P(("queue", "head"), None),
            P("head", None),
            P(),
            P(),
            P(),
            P(),
            P(None, "head"),
            P(None, "head"),
            P(None, "head"),
            P("head", None),
            P("head"),
            P("head"),
        ),
        out_specs=(P(None, ("queue", "head"), None), P(("queue", "head"), None)),
        check_vma=False,
    )
```

```python
import functools
import math

import jax
import jax.numpy as jnp
from jax import lax
from jax.experimental import pallas as pl
from jax.experimental.pallas import tpu as pltpu
from jax.sharding import PartitionSpec as P

HD = 128
STEPS = 2
COLS = 1024
TILE = 512
BEHIND = 3
MESH = pl.DeviceIdType.MESH
VMEM = pl.BlockSpec(memory_space=pltpu.VMEM)
SMEM = pl.BlockSpec(memory_space=pltpu.SMEM)
HBM = pl.BlockSpec(memory_space=pl.ANY)


def each(count, body):
    def one(i, carry):
        body(i)
        return carry

    lax.fori_loop(0, count, one, 0)


def fused_kernel(
    slots,
    heads,
    levels_ref,
    windows_ref,
    plan_ref,
    latent_ref,
    fresh_ref,
    table_ref,
    wq_ref,
    wk_ref,
    wv_ref,
    wo_ref,
    gq_ref,
    gk_ref,
    speed_ref,
    new_ref,
    state,
    mod,
    weights,
    outer,
    gathered,
    acc,
    sums,
    sums_in,
    qkv,
    held,
    results,
    attn,
    sent,
    got,
    relay,
    in_sem,
    w_sem,
    o_sem,
    own_send,
    own_recv,
    fwd_send,
    fwd_recv,
    sum_send,
    sum_recv,
    v_send,
    v_recv,
    qk_send,
    qk_recv,
    local_sem,
    back_send,
    back_recv,
    part_send,
    part_recv,
    shift_send,
    shift_recv,
):
    slot_me = lax.axis_index("queue")
    me = lax.axis_index("head")
    across = me + 1 - 2 * lax.rem(me, 2)
    along = lax.rem(me + 2, heads)
    near = (across, along)
    far = lax.rem(across + 2, heads)
    rows, width = state.shape[1:]
    chunks, part_rows = gathered.shape[1:3]
    span = 2 * part_rows
    few = rows // 2
    last = chunks - 1
    stages = 2 * chunks
    features = wq_ref.shape[1]
    heads_local = features // HD
    sources = (wq_ref, wk_ref, wv_ref)

    def block(owner):
        return pl.ds(pl.multiple_of(owner * few, few), few)

    def cols(c):
        return pl.ds(pl.multiple_of(c * COLS, COLS), COLS)

    def half(s):
        return pl.ds(s * TILE, TILE)

    load = pltpu.make_async_copy(latent_ref, state.at[0], in_sem.at[0])
    load_fresh = pltpu.make_async_copy(fresh_ref, state.at[1], in_sem.at[1])
    load.start()

    def fetch(c, m):
        at = cols(c)
        return pltpu.make_async_copy(
            sources[m].at[at, :], weights.at[m, at, :], w_sem.at[c, m]
        )

    def fetch_outer(c):
        return pltpu.make_async_copy(
            wo_ref.at[:, cols(c)], outer.at[c], o_sem.at[c]
        )

    @functools.partial(each, chunks)
    def _(c):
        for m in range(3):
            fetch(c, m).start()

    each(chunks, lambda c: fetch_outer(c).start())

    @pl.when(slot_me == slots - 1)
    def _():
        load_fresh.start()

    barrier = pltpu.get_barrier_semaphore()
    for d in range(1, heads):
        pl.semaphore_signal(
            barrier, inc=1, device_id={"head": lax.rem(me + d, heads)}, device_id_type=MESH
        )
    for d in range(1, slots):
        pl.semaphore_signal(
            barrier, inc=1, device_id={"queue": lax.rem(slot_me + d, slots)}, device_id_type=MESH
        )

    t_from = plan_ref[levels_ref[slot_me]].astype(jnp.float32)
    t_below = plan_ref[levels_ref[jnp.maximum(slot_me - 1, 0)]].astype(jnp.float32)
    t_to = jnp.where(slot_me > 0, t_below, 0.0)
    factor = (t_to - t_from) / 1000.0
    mid = width // 2
    index = lax.broadcasted_iota(jnp.int32, (1, mid), 1).astype(jnp.float32)
    angle = t_from * jnp.exp(-math.log(10000.0) * index / mid)
    for at, emb in ((slice(0, mid), jnp.cos(angle)), (slice(mid, width), jnp.sin(angle))):
        mod[0:1, at] = table_ref[0:1, at] + emb
        mod[1:2, at] = 1.0 + (table_ref[1:2, at] + emb)
        mod[2:3, at] = table_ref[2:3, at] + emb

    pl.semaphore_wait(barrier, heads - 1 + slots - 1)
    load.wait()

    def own(k, way, owner):
        piece = gathered.at[k // chunks, k % chunks, block(owner), :]
        return pltpu.make_async_remote_copy(
            src_ref=piece,
            dst_ref=piece,
            send_sem=own_send.at[k, way],
            recv_sem=own_recv.at[k, way],
            device_id={"head": near[way]},
            device_id_type=MESH,
        )

    def forward(k, s, owner):
        piece = gathered.at[k // chunks, k % chunks, block(owner), half(s)]
        return pltpu.make_async_remote_copy(
            src_ref=piece,
            dst_ref=piece,
            send_sem=fwd_send.at[k, s],
            recv_sem=fwd_recv.at[k, s],
            device_id={"head": near[1 - s]},
            device_id_type=MESH,
        )

    def share(h, d):
        return pltpu.make_async_remote_copy(
            src_ref=sums.at[h],
            dst_ref=sums_in.at[h, d - 1],
            send_sem=sum_send.at[h, d - 1],
            recv_sem=sum_recv.at[h, d - 1],
            device_id={"head": lax.rem(me + d, heads)},
            device_id_type=MESH,
        )

    def multiply(k):
        h, c = k // chunks, k % chunks

        @functools.partial(each, 3)
        def _(m):
            product = jnp.dot(
                gathered[h, c], weights[m, cols(c), :], preferred_element_type=jnp.float32
            )
            acc[h, m] = jnp.where(c == 0, product, acc[h, m] + product)

    def here(h):
        return pl.ds(pl.multiple_of(h * part_rows, part_rows), part_rows)

    def send_values(step, h):
        totals = []
        for m in range(2):
            value = acc[h, m]
            totals.append(jnp.sum(value * value, axis=-1, keepdims=True))
        wide = jnp.broadcast_to(jnp.concatenate(totals, axis=0), (span, span))
        sums[h] = jnp.transpose(wide)[:8]
        for d in range(1, heads):
            share(h, d).start()
        for j in range(heads_local):
            qkv[j, 2, here(h)] = acc[h, 2, :, j * HD : (j + 1) * HD].astype(jnp.bfloat16)

        @functools.partial(each, slots - 1)
        def _(d):
            push_v(step, h, lax.rem(slot_me + slots - 1 - d, slots), slot_me).start()

    def send_keys(step, h):
        total = sums[h]
        for d in range(1, heads):
            share(h, d).wait_recv()
            total = total + sums_in[h, d - 1]
        norm = lax.rsqrt(total / (features * heads) + 1e-06)
        column = jnp.transpose(jnp.broadcast_to(norm[:1], (span, span)))
        for m, gain_ref in ((0, gq_ref), (1, gk_ref)):
            scale = column[m * part_rows : (m + 1) * part_rows]
            if m == 0:
                scale = scale * (1.0 / (math.log(2.0) * math.sqrt(HD)))
            for j in range(heads_local):
                at = slice(j * HD, (j + 1) * HD)
                qkv[j, m, here(h)] = (acc[h, m, :, at] * scale * gain_ref[:, at]).astype(
                    jnp.bfloat16
                )

        @functools.partial(each, slots - 1)
        def _(d):
            push_qk(step, h, lax.rem(slot_me + slots - 1 - d, slots), slot_me).start()

    def rows_of(slot):
        return pl.ds(pl.multiple_of(slot * span, span), span)

    def columns_of(head):
        return pl.ds(pl.multiple_of(head * HD, HD), HD)

    def some_rows(slot, h):
        return pl.ds(pl.multiple_of(slot * span + h * part_rows, part_rows), part_rows)

    def push_v(step, h, peer, owner):
        return pltpu.make_async_remote_copy(
            src_ref=qkv.at[peer, 2, here(h), :],
            dst_ref=held.at[step, 2, some_rows(owner, h), :],
            send_sem=v_send.at[step, h, peer],
            recv_sem=v_recv.at[step, h, owner],
            device_id={"queue": peer},
            device_id_type=MESH,
        )

    def push_qk(step, h, peer, owner):
        return pltpu.make_async_remote_copy(
            src_ref=qkv.at[peer, 0:2, here(h), :],
            dst_ref=held.at[step, 0:2, some_rows(owner, h), :],
            send_sem=qk_send.at[step, h, peer],
            recv_sem=qk_recv.at[step, h, owner],
            device_id={"queue": peer},
            device_id_type=MESH,
        )

    def give(step, h, peer, head):
        return pltpu.make_async_remote_copy(
            src_ref=results.at[peer, here(h), :],
            dst_ref=attn.at[here(h), columns_of(head)],
            send_sem=back_send.at[step, h, peer],
            recv_sem=back_recv.at[step, h, head],
            device_id={"queue": peer},
            device_id_type=MESH,
        )

    def part(k, s, kind):
        target = near[s] if kind < 2 else near[1 - s]
        if kind == 0:
            source = sent.at[k, block(far), half(s)]
        elif kind == 1:
            source = sent.at[k, block(near[s]), half(s)]
        else:
            source = relay.at[k, s]
        return pltpu.make_async_remote_copy(
            src_ref=source,
            dst_ref=got.at[k, s, kind],
            send_sem=part_send.at[k, s, kind],
            recv_sem=part_recv.at[k, s, kind],
            device_id={"head": target},
            device_id_type=MESH,
        )

    def strip(k):
        return pl.ds(pl.multiple_of(k // chunks * few, few), few)

    def hand_down(k, peer):
        at = cols(k % chunks)
        return pltpu.make_async_remote_copy(
            src_ref=new_ref.at[strip(k), at],
            dst_ref=state.at[1, strip(k), at],
            send_sem=shift_send.at[k],
            recv_sem=shift_recv.at[k],
            device_id={"queue": peer},
            device_id_type=MESH,
        )

    above = lax.rem(slot_me + 1, slots)
    below = lax.rem(slot_me + slots - 1, slots)

    @functools.partial(each, STEPS)
    def _(step):
        x = state[step].astype(jnp.float32)
        mean = jnp.mean(x, axis=-1, keepdims=True)
        var = jnp.mean((x - mean) ** 2, axis=-1, keepdims=True)
        inv = lax.rsqrt(var + 1e-06)

        @functools.partial(each, chunks)
        def _(c):
            piece = state[step, :, cols(c)].astype(jnp.float32)
            normed = (piece - mean) * inv * mod[1:2, cols(c)] + mod[0:1, cols(c)]
            for h in range(2):
                gathered[h, c, block(me), :] = normed[h * few : (h + 1) * few].astype(
                    jnp.bfloat16
                )
            own(c, 0, me).start()
            own(c, 1, me).start()

        @functools.partial(each, stages + BEHIND)
        def _(k):
            @pl.when(k < stages)
            def _():
                own(k, 0, across).wait_recv()
                forward(k, 0, across).start()
                own(k, 1, along).wait_recv()
                forward(k, 1, along).start()

            @pl.when(k < chunks)
            def _():
                own(k + chunks, 0, me).start()
                own(k + chunks, 1, me).start()

            at = k - BEHIND

            @pl.when(at >= 0)
            def _():
                forward(at, 0, far).wait_recv()
                forward(at, 1, far).wait_recv()

                @pl.when((step == 0) & (at < chunks))
                def _():
                    for m in range(3):
                        fetch(at, m).wait()

                multiply(at)

                @pl.when(at % chunks == last)
                def _():
                    send_values(step, at // chunks)

                @pl.when((at == chunks + 1) | (at == stages - 1))
                def _():
                    send_keys(step, at // stages + (at + 1) // stages)

        keep = pltpu.make_async_copy(
            qkv.at[slot_me], held.at[step, :, rows_of(slot_me), :], local_sem.at[0]
        )
        keep.start()
        for h in range(2):
            for d in range(1, heads):
                share(h, d).wait_send()

        @functools.partial(each, stages)
        def _(k):
            for s in range(2):
                own(k, s, me).wait_send()
                forward(k, s, near[s]).wait_send()

        keep.wait()

        settle = pltpu.make_async_copy(
            results.at[slot_me], attn.at[:, columns_of(slot_me)], local_sem.at[1]
        )
        for pair in range(0, slots, 2):
            group = range(pair, min(pair + 2, slots))
            for slot in group:

                @pl.when(slot_me != slot)
                def _(slot=slot):
                    for h in range(2):
                        push_v(step, h, slot, slot).wait_recv()
                        push_qk(step, h, slot, slot).wait_recv()

            end = group[-1] * span + span
            scores = lax.dot_general(
                held[step, 0, pair * span : end, :],
                held[step, 1, :end, :],
                (((1,), (1,)), ((), ())),
                preferred_element_type=jnp.float32,
            )
            for slot in group:
                count = (slot + 1) * span
                at = (slot - pair) * span
                ids = lax.broadcasted_iota(jnp.int32, (1, count), 1)
                valid = ids >= (slot - windows_ref[slot] + 1) * span
                masked = jnp.where(valid, scores[at : at + span, :count], -1e30)
                top = jnp.max(masked, axis=-1, keepdims=True)
                soft = jnp.exp2(masked - top)
                total = jnp.sum(soft, axis=-1, keepdims=True)
                summed = jnp.dot(
                    soft.astype(jnp.bfloat16),
                    held[step, 2, :count, :],
                    preferred_element_type=jnp.float32,
                )
                results[slot] = (summed / total).astype(jnp.bfloat16)
            for slot in group:

                @pl.when(slot_me != slot)
                def _(slot=slot):
                    give(step, 0, slot, slot_me).start()

                @pl.when(slot_me == slot)
                def _():
                    settle.start()

        @functools.partial(each, slots)
        def _(slot):
            @pl.when(slot_me != slot)
            def _():
                give(step, 1, slot, slot_me).start()

        settle.wait()

        def relay_part(k):
            for s in range(2):
                part(k, s, 0).wait_recv()
                both = sent[k, block(near[1 - s]), half(s)].astype(jnp.float32) + got[
                    k, s, 0
                ].astype(jnp.float32)
                relay[k, s] = both.astype(jnp.bfloat16)
                part(k, s, 2).start()

        def finish(k):
            for s in range(2):
                at = pl.ds(pl.multiple_of(k % chunks * COLS + s * TILE, TILE), TILE)
                part(k, s, 1).wait_recv()
                part(k, s, 2).wait_recv()
                total = (
                    sent[k, block(me), half(s)].astype(jnp.float32)
                    + got[k, s, 1].astype(jnp.float32)
                    + got[k, s, 2].astype(jnp.float32)
                )
                before = state[step, strip(k), at].astype(jnp.float32)
                speed = (before + mod[2:3, at] * total).astype(jnp.bfloat16)
                speed_ref[step, strip(k), at] = speed
                new_ref[strip(k), at] = (before + factor * speed.astype(jnp.float32)).astype(
                    jnp.bfloat16
                )

            @pl.when((step < STEPS - 1) & (slot_me > 0))
            def _():
                hand_down(k, below).start()

        @functools.partial(each, stages + 2)
        def _(k):
            @pl.when(k < stages)
            def _():
                @pl.when(k % chunks == 0)
                def _():
                    @functools.partial(each, slots)
                    def _(slot):
                        @pl.when(slot_me != slot)
                        def _():
                            give(step, k // chunks, slot, slot).wait_recv()

                @pl.when((step == 0) & (k < chunks))
                def _():
                    fetch_outer(k).wait()

                sent[k] = jnp.dot(
                    attn[here(k // chunks), :],
                    outer[k % chunks],
                    preferred_element_type=jnp.float32,
                ).astype(jnp.bfloat16)
                for s in range(2):
                    part(k, s, 0).start()
                    part(k, s, 1).start()

            @pl.when((k > 0) & (k <= stages))
            def _():
                relay_part(k - 1)

            @pl.when(k > 1)
            def _():
                finish(k - 2)

        @functools.partial(each, stages)
        def _(k):
            for s in range(2):
                for kind in range(3):
                    part(k, s, kind).wait_send()

        @functools.partial(each, slots)
        def _(slot):
            @pl.when(slot_me != slot)
            def _():
                for h in range(2):
                    push_v(step, h, slot, slot_me).wait_send()
                    push_qk(step, h, slot, slot_me).wait_send()
                    give(step, h, slot, slot_me).wait_send()

        @pl.when(step < STEPS - 1)
        def _():
            @pl.when(slot_me > 0)
            def _():
                each(stages, lambda k: hand_down(k, below).wait_send())

            @pl.when(slot_me < slots - 1)
            def _():
                each(stages, lambda k: hand_down(k, above).wait_recv())

            @pl.when(slot_me == slots - 1)
            def _():
                load_fresh.wait()


def fused(
    latent, fresh, levels, windows, plan, table, wq, wk, wv, wo, gq, gk, slots, heads
):
    rows, width = latent.shape
    span, features = rows * heads, wq.shape[1]
    chunks, heads_local = width // COLS, features // HD
    dma = pltpu.SemaphoreType.DMA
    bf16, f32 = jnp.bfloat16, jnp.float32
    return pl.pallas_call(
        functools.partial(fused_kernel, slots, heads),
        out_shape=(
            jax.ShapeDtypeStruct((STEPS, rows, width), bf16),
            jax.ShapeDtypeStruct((rows, width), bf16),
        ),
        in_specs=[SMEM] * 3 + [HBM] * 2 + [VMEM] + [HBM] * 4 + [VMEM] * 2,
        out_specs=(VMEM, VMEM),
        scratch_shapes=[
            pltpu.VMEM((STEPS, rows, width), bf16),
            pltpu.VMEM((3, width), f32),
            pltpu.VMEM((3, width, features), bf16),
            pltpu.VMEM((chunks, features, COLS), bf16),
            pltpu.VMEM((2, chunks, span // 2, COLS), bf16),
            pltpu.VMEM((2, 3, span // 2, features), f32),
            pltpu.VMEM((2, 8, span), f32),
            pltpu.VMEM((2, heads - 1, 8, span), f32),
            pltpu.VMEM((heads_local, 3, span, HD), bf16),
            pltpu.VMEM((STEPS, 3, slots * span, HD), bf16),
            pltpu.VMEM((slots, span, HD), bf16),
            pltpu.VMEM((span, features), bf16),
            pltpu.VMEM((2 * chunks, span // 2, COLS), bf16),
            pltpu.VMEM((2 * chunks, 2, 3, rows // 2, TILE), bf16),
            pltpu.VMEM((2 * chunks, 2, rows // 2, TILE), bf16),
            dma((2,)),
            dma((chunks, 3)),
            dma((chunks,)),
            dma((2 * chunks, 2)),
            dma((2 * chunks, 2)),
            dma((2 * chunks, 2)),
            dma((2 * chunks, 2)),
            dma((2, heads - 1)),
            dma((2, heads - 1)),
            dma((STEPS, 2, slots)),
            dma((STEPS, 2, slots)),
            dma((STEPS, 2, slots)),
            dma((STEPS, 2, slots)),
            dma((2,)),
            dma((STEPS, 2, slots)),
            dma((STEPS, 2, slots)),
            dma((2 * chunks, 2, 3)),
            dma((2 * chunks, 2, 3)),
            dma((2 * chunks,)),
            dma((2 * chunks,)),
        ],
        compiler_params=pltpu.CompilerParams(
            collective_id=0, has_side_effects=True, vmem_limit_bytes=54 * 2**20
        ),
        cost_estimate=pl.CostEstimate(
            flops=STEPS * 8 * span * width * features,
            bytes_accessed=8 * width * features,
            transcendentals=0,
        ),
        name="denoise",
    )(levels, windows, plan, latent, fresh, table, wq, wk, wv, wo, gq, gk)


def shifted(array, axis, by):
    length = lax.axis_size(axis)
    pairs = [(i, i + by) for i in range(length) if 0 <= i + by < length]
    return lax.ppermute(array, axis, pairs)


def embed(times, width):
    half = width // 2
    freq = jnp.exp(-math.log(10000.0) * jnp.arange(half, dtype=jnp.float32) / half)
    angle = times[:, None] * freq[None, :]
    return jnp.concatenate([jnp.cos(angle), jnp.sin(angle)], axis=-1)


def absorb(carry, keys, values, first_row, queries, lower, slot, span):
    top, total, summed = carry
    count = keys.shape[0]
    heads_local = keys.shape[1] // HD
    key_heads = keys.reshape(count, heads_local, HD)
    value_heads = values.reshape(count, heads_local, HD)
    scores = jnp.einsum(
        "qhd,khd->hqk", queries, key_heads, preferred_element_type=jnp.float32
    ) / math.sqrt(HD)
    span_ids = (first_row + jnp.arange(count, dtype=jnp.int32)) // span
    valid = ((span_ids >= lower) & (span_ids <= slot))[None, None, :]
    masked = jnp.where(valid, scores, -1e30)
    new_top = jnp.maximum(top, jnp.max(masked, axis=-1))
    weights = jnp.where(valid, jnp.exp(scores - new_top[:, :, None]), 0.0)
    fade = jnp.exp(top - new_top)
    total = total * fade + jnp.sum(weights, axis=-1)
    summed = summed * fade[:, :, None] + jnp.einsum(
        "hqk,khd->hqd",
        weights.astype(jnp.bfloat16),
        value_heads,
        preferred_element_type=jnp.float32,
    )
    return (new_top, total, summed)


def on_device(
    latent,
    fresh,
    levels,
    windows,
    plan,
    mod_table,
    w_query,
    w_key,
    w_value,
    w_out,
    query_gain,
    key_gain,
):
    queue_count = lax.axis_size("queue")
    head_count = lax.axis_size("head")
    slot = lax.axis_index("queue")
    rows = latent.shape[0]
    span = rows * head_count
    features = w_query.shape[1]
    heads_local = features // HD
    fits = latent.shape[1] % COLS == 0 and features % TILE == 0 and COLS == 2 * TILE
    if queue_count == heads_local and head_count == 4 and span == HD and rows % 32 == 0 and fits:
        return fused(
            latent,
            fresh,
            levels,
            windows,
            plan,
            mod_table,
            w_query,
            w_key,
            w_value,
            w_out,
            query_gain[None],
            key_gain[None],
            queue_count,
            head_count,
        )
    table_hits = levels[:, None] == jnp.arange(plan.shape[0], dtype=jnp.int32)[None, :]
    t_all = jnp.sum(jnp.where(table_hits, plan[None, :], 0), axis=1).astype(jnp.float32)
    t_from = t_all[slot]
    t_to = jnp.where(slot > 0, t_all[jnp.maximum(slot - 1, 0)], 0.0)
    step_size = (t_to - t_from) / 1000.0
    lower = jnp.maximum(0, slot - windows[slot] + 1)
    emb = embed(t_from[None], latent.shape[1])[0]
    shift = mod_table[0] + emb
    scale = mod_table[1] + emb
    gate = mod_table[2] + emb
    state = latent
    speeds = []
    new = latent
    for step in range(STEPS):
        x = state.astype(jnp.float32)
        mean = jnp.mean(x, axis=-1, keepdims=True)
        var = jnp.mean((x - mean) ** 2, axis=-1, keepdims=True)
        normed = ((x - mean) * lax.rsqrt(var + 1e-06) * (1.0 + scale) + shift).astype(jnp.bfloat16)
        piece = lax.all_gather(normed, "head", axis=0, tiled=True)
        projected = jnp.concatenate(
            [
                jnp.dot(piece, w_query, preferred_element_type=jnp.float32),
                jnp.dot(piece, w_key, preferred_element_type=jnp.float32),
                jnp.dot(piece, w_value, preferred_element_type=jnp.float32),
            ],
            axis=-1,
        )
        q = projected[:, :features]
        k = projected[:, features : 2 * features]
        values = projected[:, 2 * features :].astype(jnp.bfloat16)
        query_sq, key_sq = lax.psum((jnp.sum(q * q, axis=-1), jnp.sum(k * k, axis=-1)), "head")
        every = features * head_count
        queries = (q * lax.rsqrt(query_sq / every + 1e-06)[:, None] * query_gain).astype(
            jnp.bfloat16
        )
        keys = (k * lax.rsqrt(key_sq / every + 1e-06)[:, None] * key_gain).astype(jnp.bfloat16)
        query_heads = queries.reshape(span, heads_local, HD)
        start_carry = (
            jnp.full((heads_local, span), -1e30, jnp.float32),
            jnp.zeros((heads_local, span), jnp.float32),
            jnp.zeros((heads_local, span, HD), jnp.float32),
        )
        inner = start_carry
        piece_keys = lax.all_gather(keys, "queue", axis=0, tiled=True)
        piece_values = lax.all_gather(values, "queue", axis=0, tiled=True)
        count = piece_keys.shape[0]
        blocks = count // span

        def one_block(running, block):
            block_keys, block_values, block_index = block
            return (
                absorb(
                    running,
                    block_keys,
                    block_values,
                    block_index * span,
                    query_heads,
                    lower,
                    slot,
                    span,
                ),
                None,
            )

        inner, unused = lax.scan(
            one_block,
            inner,
            (
                piece_keys.reshape(blocks, span, features),
                piece_values.reshape(blocks, span, features),
                jnp.arange(blocks, dtype=jnp.int32),
            ),
        )
        top, total, summed = inner
        attn = (
            jnp.transpose(summed / total[:, :, None], (1, 0, 2))
            .reshape(span, features)
            .astype(jnp.bfloat16)
        )
        mixed = lax.psum_scatter(
            jnp.dot(attn, w_out, preferred_element_type=jnp.float32).astype(jnp.bfloat16),
            "head",
            scatter_dimension=0,
            tiled=True,
        ).astype(jnp.float32)
        speed = (x + gate * mixed).astype(jnp.bfloat16)
        speeds.append(speed)
        new = (x + step_size * speed.astype(jnp.float32)).astype(jnp.bfloat16)
        if step < STEPS - 1:
            moved = shifted(new, "queue", -1)
            state = jnp.where(slot == queue_count - 1, fresh, moved)
    return (jnp.stack(speeds), new)


def solution(mesh):
    return jax.shard_map(
        on_device,
        mesh=mesh,
        in_specs=(
            P(("queue", "head"), None),
            P("head", None),
            P(),
            P(),
            P(),
            P(),
            P(None, "head"),
            P(None, "head"),
            P(None, "head"),
            P("head", None),
            P("head"),
            P("head"),
        ),
        out_specs=(P(None, ("queue", "head"), None), P(("queue", "head"), None)),
        check_vma=False,
    )
```

```python
import functools
import math

import jax
import jax.numpy as jnp
from jax import lax
from jax.experimental import pallas as pl
from jax.experimental.pallas import tpu as pltpu
from jax.sharding import PartitionSpec as P

HD = 128
STEPS = 2
COLS = 2560
TILE = 1280
BEHIND = 1
MESH = pl.DeviceIdType.MESH
VMEM = pl.BlockSpec(memory_space=pltpu.VMEM)
SMEM = pl.BlockSpec(memory_space=pltpu.SMEM)
HBM = pl.BlockSpec(memory_space=pl.ANY)


def each(count, body):
    def one(i, carry):
        body(i)
        return carry

    lax.fori_loop(0, count, one, 0)


def fused_kernel(
    slots,
    heads,
    levels_ref,
    windows_ref,
    plan_ref,
    latent_ref,
    fresh_ref,
    table_ref,
    wq_ref,
    wk_ref,
    wv_ref,
    wo_ref,
    gq_ref,
    gk_ref,
    speed_ref,
    new_ref,
    state,
    mod,
    weights,
    outer,
    gathered,
    acc,
    sums,
    sums_in,
    qkv,
    held,
    results,
    attn,
    sent,
    got,
    relay,
    in_sem,
    w_sem,
    o_sem,
    own_send,
    own_recv,
    fwd_send,
    fwd_recv,
    sum_send,
    sum_recv,
    qkv_send,
    qkv_recv,
    local_sem,
    back_send,
    back_recv,
    part_send,
    part_recv,
    shift_send,
    shift_recv,
):
    slot_me = lax.axis_index("queue")
    me = lax.axis_index("head")
    across = me + 1 - 2 * lax.rem(me, 2)
    along = lax.rem(me + 2, heads)
    near = (across, along)
    far = lax.rem(across + 2, heads)
    rows, width = state.shape[1:]
    chunks, part_rows = gathered.shape[1:3]
    span = 2 * part_rows
    few = rows // 2
    last = chunks - 1
    stages = 2 * chunks
    features = wq_ref.shape[1]
    heads_local = features // HD
    sources = (wq_ref, wk_ref, wv_ref)

    def block(owner):
        return pl.ds(pl.multiple_of(owner * few, few), few)

    def cols(c):
        return pl.ds(pl.multiple_of(c * COLS, COLS), COLS)

    def half(s):
        return pl.ds(s * TILE, TILE)

    load = pltpu.make_async_copy(latent_ref, state.at[0], in_sem.at[0])
    load_fresh = pltpu.make_async_copy(fresh_ref, state.at[1], in_sem.at[1])
    load.start()

    def fetch(c, m):
        at = cols(c)
        return pltpu.make_async_copy(
            sources[m].at[at, :], weights.at[m, at, :], w_sem.at[c, m]
        )

    def fetch_outer(c):
        return pltpu.make_async_copy(
            wo_ref.at[:, cols(c)], outer.at[c], o_sem.at[c]
        )

    @functools.partial(each, chunks)
    def _(c):
        for m in range(3):
            fetch(c, m).start()

    each(chunks, lambda c: fetch_outer(c).start())

    @pl.when(slot_me == slots - 1)
    def _():
        load_fresh.start()

    barrier = pltpu.get_barrier_semaphore()
    for d in range(1, heads):
        pl.semaphore_signal(
            barrier, inc=1, device_id={"head": lax.rem(me + d, heads)}, device_id_type=MESH
        )
    for d in range(1, slots):
        pl.semaphore_signal(
            barrier, inc=1, device_id={"queue": lax.rem(slot_me + d, slots)}, device_id_type=MESH
        )

    t_from = plan_ref[levels_ref[slot_me]].astype(jnp.float32)
    t_below = plan_ref[levels_ref[jnp.maximum(slot_me - 1, 0)]].astype(jnp.float32)
    t_to = jnp.where(slot_me > 0, t_below, 0.0)
    factor = (t_to - t_from) / 1000.0
    mid = width // 2
    index = lax.broadcasted_iota(jnp.int32, (1, mid), 1).astype(jnp.float32)
    angle = t_from * jnp.exp(-math.log(10000.0) * index / mid)
    for at, emb in ((slice(0, mid), jnp.cos(angle)), (slice(mid, width), jnp.sin(angle))):
        mod[0:1, at] = table_ref[0:1, at] + emb
        mod[1:2, at] = 1.0 + (table_ref[1:2, at] + emb)
        mod[2:3, at] = table_ref[2:3, at] + emb

    pl.semaphore_wait(barrier, heads - 1 + slots - 1)
    load.wait()

    def own(k, way, owner):
        piece = gathered.at[k // chunks, k % chunks, block(owner), :]
        return pltpu.make_async_remote_copy(
            src_ref=piece,
            dst_ref=piece,
            send_sem=own_send.at[k, way],
            recv_sem=own_recv.at[k, way],
            device_id={"head": near[way]},
            device_id_type=MESH,
        )

    def forward(k, s, owner):
        piece = gathered.at[k // chunks, k % chunks, block(owner), half(s)]
        return pltpu.make_async_remote_copy(
            src_ref=piece,
            dst_ref=piece,
            send_sem=fwd_send.at[k, s],
            recv_sem=fwd_recv.at[k, s],
            device_id={"head": near[1 - s]},
            device_id_type=MESH,
        )

    def share(h, d):
        return pltpu.make_async_remote_copy(
            src_ref=sums.at[h],
            dst_ref=sums_in.at[h, d - 1],
            send_sem=sum_send.at[h, d - 1],
            recv_sem=sum_recv.at[h, d - 1],
            device_id={"head": lax.rem(me + d, heads)},
            device_id_type=MESH,
        )

    def multiply(k):
        h, c = k // chunks, k % chunks

        @functools.partial(each, 3)
        def _(m):
            product = jnp.dot(
                gathered[h, c], weights[m, cols(c), :], preferred_element_type=jnp.float32
            )
            acc[h, m] = jnp.where(c == 0, product, acc[h, m] + product)

    def here(h):
        return pl.ds(pl.multiple_of(h * part_rows, part_rows), part_rows)

    def send_sums(h):
        totals = []
        for m in range(2):
            value = acc[h, m]
            totals.append(jnp.sum(value * value, axis=-1, keepdims=True))
        wide = jnp.broadcast_to(jnp.concatenate(totals, axis=0), (span, span))
        sums[h] = jnp.transpose(wide)[:8]
        for d in range(1, heads):
            share(h, d).start()
        for j in range(heads_local):
            qkv[j, 2, here(h)] = acc[h, 2, :, j * HD : (j + 1) * HD].astype(jnp.bfloat16)

    def send_keys(step, h):
        total = sums[h]
        for d in range(1, heads):
            share(h, d).wait_recv()
            total = total + sums_in[h, d - 1]
        norm = lax.rsqrt(total / (features * heads) + 1e-06)
        column = jnp.transpose(jnp.broadcast_to(norm[:1], (span, span)))
        for m, gain_ref in ((0, gq_ref), (1, gk_ref)):
            scale = column[m * part_rows : (m + 1) * part_rows]
            if m == 0:
                scale = scale * (1.0 / (math.log(2.0) * math.sqrt(HD)))
            for j in range(heads_local):
                at = slice(j * HD, (j + 1) * HD)
                qkv[j, m, here(h)] = (acc[h, m, :, at] * scale * gain_ref[:, at]).astype(
                    jnp.bfloat16
                )

        @functools.partial(each, slots - 1)
        def _(d):
            push(step, h, lax.rem(slot_me + slots - 1 - d, slots), slot_me).start()

    def rows_of(slot):
        return pl.ds(pl.multiple_of(slot * span, span), span)

    def columns_of(head):
        return pl.ds(pl.multiple_of(head * HD, HD), HD)

    def some_rows(slot, h):
        return pl.ds(pl.multiple_of(slot * span + h * part_rows, part_rows), part_rows)

    def push(step, h, peer, owner):
        return pltpu.make_async_remote_copy(
            src_ref=qkv.at[peer, :, here(h), :],
            dst_ref=held.at[step, :, some_rows(owner, h), :],
            send_sem=qkv_send.at[step, h, peer],
            recv_sem=qkv_recv.at[step, h, owner],
            device_id={"queue": peer},
            device_id_type=MESH,
        )

    def give(step, peer, head):
        return pltpu.make_async_remote_copy(
            src_ref=results.at[peer],
            dst_ref=attn.at[:, columns_of(head)],
            send_sem=back_send.at[step, peer],
            recv_sem=back_recv.at[step, head],
            device_id={"queue": peer},
            device_id_type=MESH,
        )

    def part(c, s, kind):
        target = near[s] if kind < 2 else near[1 - s]
        if kind == 0:
            source = sent.at[c, :, block(far), half(s)]
        elif kind == 1:
            source = sent.at[c, :, block(near[s]), half(s)]
        else:
            source = relay.at[c, s]
        return pltpu.make_async_remote_copy(
            src_ref=source,
            dst_ref=got.at[c, s, kind],
            send_sem=part_send.at[c, s, kind],
            recv_sem=part_recv.at[c, s, kind],
            device_id={"head": target},
            device_id_type=MESH,
        )

    def hand_down(c, peer):
        at = cols(c)
        return pltpu.make_async_remote_copy(
            src_ref=new_ref.at[:, at],
            dst_ref=state.at[1, :, at],
            send_sem=shift_send.at[c],
            recv_sem=shift_recv.at[c],
            device_id={"queue": peer},
            device_id_type=MESH,
        )

    above = lax.rem(slot_me + 1, slots)
    below = lax.rem(slot_me + slots - 1, slots)

    @functools.partial(each, STEPS)
    def _(step):
        x = state[step].astype(jnp.float32)
        mean = jnp.mean(x, axis=-1, keepdims=True)
        var = jnp.mean((x - mean) ** 2, axis=-1, keepdims=True)
        inv = lax.rsqrt(var + 1e-06)

        @functools.partial(each, chunks)
        def _(c):
            piece = state[step, :, cols(c)].astype(jnp.float32)
            normed = (piece - mean) * inv * mod[1:2, cols(c)] + mod[0:1, cols(c)]
            for h in range(2):
                gathered[h, c, block(me), :] = normed[h * few : (h + 1) * few].astype(
                    jnp.bfloat16
                )
            own(c, 0, me).start()
            own(c, 1, me).start()

        @functools.partial(each, stages + BEHIND)
        def _(k):
            @pl.when(k < stages)
            def _():
                own(k, 0, across).wait_recv()
                forward(k, 0, across).start()
                own(k, 1, along).wait_recv()
                forward(k, 1, along).start()

            @pl.when(k < chunks)
            def _():
                own(k + chunks, 0, me).start()
                own(k + chunks, 1, me).start()

            at = k - BEHIND

            @pl.when(at >= 0)
            def _():
                forward(at, 0, far).wait_recv()
                forward(at, 1, far).wait_recv()

                @pl.when((step == 0) & (at < chunks))
                def _():
                    for m in range(3):
                        fetch(at, m).wait()

                multiply(at)

                @pl.when(at % chunks == last)
                def _():
                    send_sums(at // chunks)

                @pl.when((at == chunks) | (at == stages - 1))
                def _():
                    send_keys(step, at // stages + (at + 1) // stages)

        keep = pltpu.make_async_copy(
            qkv.at[slot_me], held.at[step, :, rows_of(slot_me), :], local_sem.at[0]
        )
        keep.start()
        for h in range(2):
            for d in range(1, heads):
                share(h, d).wait_send()

        @functools.partial(each, stages)
        def _(k):
            for s in range(2):
                own(k, s, me).wait_send()
                forward(k, s, near[s]).wait_send()

        keep.wait()

        settle = pltpu.make_async_copy(
            results.at[slot_me], attn.at[:, columns_of(slot_me)], local_sem.at[1]
        )
        for pair in range(0, slots, 2):
            group = range(pair, min(pair + 2, slots))
            for slot in group:

                @pl.when(slot_me != slot)
                def _(slot=slot):
                    for h in range(2):
                        push(step, h, slot, slot).wait_recv()

            end = group[-1] * span + span
            scores = lax.dot_general(
                held[step, 0, pair * span : end, :],
                held[step, 1, :end, :],
                (((1,), (1,)), ((), ())),
                preferred_element_type=jnp.float32,
            )
            for slot in group:
                count = (slot + 1) * span
                at = (slot - pair) * span
                ids = lax.broadcasted_iota(jnp.int32, (1, count), 1)
                valid = ids >= (slot - windows_ref[slot] + 1) * span
                masked = jnp.where(valid, scores[at : at + span, :count], -1e30)
                top = jnp.max(masked, axis=-1, keepdims=True)
                soft = jnp.exp2(masked - top)
                total = jnp.sum(soft, axis=-1, keepdims=True)
                summed = jnp.dot(
                    soft.astype(jnp.bfloat16),
                    held[step, 2, :count, :],
                    preferred_element_type=jnp.float32,
                )
                results[slot] = (summed / total).astype(jnp.bfloat16)
            for slot in group:

                @pl.when(slot_me != slot)
                def _(slot=slot):
                    give(step, slot, slot_me).start()

                @pl.when(slot_me == slot)
                def _():
                    settle.start()

        settle.wait()

        @functools.partial(each, slots)
        def _(slot):
            @pl.when(slot_me != slot)
            def _():
                give(step, slot, slot).wait_recv()

        def relay_part(c):
            for s in range(2):
                part(c, s, 0).wait_recv()
                both = sent[c, :, block(near[1 - s]), half(s)].astype(jnp.float32) + got[
                    c, s, 0
                ].astype(jnp.float32)
                relay[c, s] = both.astype(jnp.bfloat16)
                part(c, s, 2).start()

        def finish(c):
            for s in range(2):
                at = pl.ds(pl.multiple_of(c * COLS + s * TILE, TILE), TILE)
                part(c, s, 1).wait_recv()
                part(c, s, 2).wait_recv()
                total = (
                    sent[c, :, block(me), half(s)].astype(jnp.float32)
                    + got[c, s, 1].astype(jnp.float32)
                    + got[c, s, 2].astype(jnp.float32)
                )
                total = total.reshape(rows, TILE)
                before = state[step, :, at].astype(jnp.float32)
                speed = (before + mod[2:3, at] * total).astype(jnp.bfloat16)
                speed_ref[step, :, at] = speed
                new_ref[:, at] = (before + factor * speed.astype(jnp.float32)).astype(
                    jnp.bfloat16
                )

            @pl.when((step < STEPS - 1) & (slot_me > 0))
            def _():
                hand_down(c, below).start()

        @functools.partial(each, chunks + 2)
        def _(c):
            @pl.when(c < chunks)
            def _():
                @pl.when(step == 0)
                def _():
                    fetch_outer(c).wait()

                for s in range(2):
                    product = jnp.dot(
                        attn[...],
                        outer[c, :, s * TILE : (s + 1) * TILE],
                        preferred_element_type=jnp.float32,
                    ).astype(jnp.bfloat16)
                    for h in range(2):
                        sent[c, h, :, s * TILE : (s + 1) * TILE] = product[
                            h * part_rows : (h + 1) * part_rows
                        ]
                    part(c, s, 0).start()
                    part(c, s, 1).start()

            @pl.when((c > 0) & (c <= chunks))
            def _():
                relay_part(c - 1)

            @pl.when(c > 1)
            def _():
                finish(c - 2)

        @functools.partial(each, chunks)
        def _(c):
            for s in range(2):
                for kind in range(3):
                    part(c, s, kind).wait_send()

        @functools.partial(each, slots)
        def _(slot):
            @pl.when(slot_me != slot)
            def _():
                for h in range(2):
                    push(step, h, slot, slot_me).wait_send()
                give(step, slot, slot_me).wait_send()

        @pl.when(step < STEPS - 1)
        def _():
            @pl.when(slot_me > 0)
            def _():
                each(chunks, lambda c: hand_down(c, below).wait_send())

            @pl.when(slot_me < slots - 1)
            def _():
                each(chunks, lambda c: hand_down(c, above).wait_recv())

            @pl.when(slot_me == slots - 1)
            def _():
                load_fresh.wait()


def fused(
    latent, fresh, levels, windows, plan, table, wq, wk, wv, wo, gq, gk, slots, heads
):
    rows, width = latent.shape
    span, features = rows * heads, wq.shape[1]
    chunks, heads_local = width // COLS, features // HD
    dma = pltpu.SemaphoreType.DMA
    bf16, f32 = jnp.bfloat16, jnp.float32
    return pl.pallas_call(
        functools.partial(fused_kernel, slots, heads),
        out_shape=(
            jax.ShapeDtypeStruct((STEPS, rows, width), bf16),
            jax.ShapeDtypeStruct((rows, width), bf16),
        ),
        in_specs=[SMEM] * 3 + [HBM] * 2 + [VMEM] + [HBM] * 4 + [VMEM] * 2,
        out_specs=(VMEM, VMEM),
        scratch_shapes=[
            pltpu.VMEM((STEPS, rows, width), bf16),
            pltpu.VMEM((3, width), f32),
            pltpu.VMEM((3, width, features), bf16),
            pltpu.VMEM((chunks, features, COLS), bf16),
            pltpu.VMEM((2, chunks, span // 2, COLS), bf16),
            pltpu.VMEM((2, 3, span // 2, features), f32),
            pltpu.VMEM((2, 8, span), f32),
            pltpu.VMEM((2, heads - 1, 8, span), f32),
            pltpu.VMEM((heads_local, 3, span, HD), bf16),
            pltpu.VMEM((STEPS, 3, slots * span, HD), bf16),
            pltpu.VMEM((slots, span, HD), bf16),
            pltpu.VMEM((span, features), bf16),
            pltpu.VMEM((chunks, 2, span // 2, COLS), bf16),
            pltpu.VMEM((chunks, 2, 3, 2, rows // 2, TILE), bf16),
            pltpu.VMEM((chunks, 2, 2, rows // 2, TILE), bf16),
            dma((2,)),
            dma((chunks, 3)),
            dma((chunks,)),
            dma((2 * chunks, 2)),
            dma((2 * chunks, 2)),
            dma((2 * chunks, 2)),
            dma((2 * chunks, 2)),
            dma((2, heads - 1)),
            dma((2, heads - 1)),
            dma((STEPS, 2, slots)),
            dma((STEPS, 2, slots)),
            dma((2,)),
            dma((STEPS, slots)),
            dma((STEPS, slots)),
            dma((chunks, 2, 3)),
            dma((chunks, 2, 3)),
            dma((chunks,)),
            dma((chunks,)),
        ],
        compiler_params=pltpu.CompilerParams(
            collective_id=0, has_side_effects=True, vmem_limit_bytes=54 * 2**20
        ),
        cost_estimate=pl.CostEstimate(
            flops=STEPS * 8 * span * width * features,
            bytes_accessed=8 * width * features,
            transcendentals=0,
        ),
        name="denoise",
    )(levels, windows, plan, latent, fresh, table, wq, wk, wv, wo, gq, gk)


def shifted(array, axis, by):
    length = lax.axis_size(axis)
    pairs = [(i, i + by) for i in range(length) if 0 <= i + by < length]
    return lax.ppermute(array, axis, pairs)


def embed(times, width):
    half = width // 2
    freq = jnp.exp(-math.log(10000.0) * jnp.arange(half, dtype=jnp.float32) / half)
    angle = times[:, None] * freq[None, :]
    return jnp.concatenate([jnp.cos(angle), jnp.sin(angle)], axis=-1)


def absorb(carry, keys, values, first_row, queries, lower, slot, span):
    top, total, summed = carry
    count = keys.shape[0]
    heads_local = keys.shape[1] // HD
    key_heads = keys.reshape(count, heads_local, HD)
    value_heads = values.reshape(count, heads_local, HD)
    scores = jnp.einsum(
        "qhd,khd->hqk", queries, key_heads, preferred_element_type=jnp.float32
    ) / math.sqrt(HD)
    span_ids = (first_row + jnp.arange(count, dtype=jnp.int32)) // span
    valid = ((span_ids >= lower) & (span_ids <= slot))[None, None, :]
    masked = jnp.where(valid, scores, -1e30)
    new_top = jnp.maximum(top, jnp.max(masked, axis=-1))
    weights = jnp.where(valid, jnp.exp(scores - new_top[:, :, None]), 0.0)
    fade = jnp.exp(top - new_top)
    total = total * fade + jnp.sum(weights, axis=-1)
    summed = summed * fade[:, :, None] + jnp.einsum(
        "hqk,khd->hqd",
        weights.astype(jnp.bfloat16),
        value_heads,
        preferred_element_type=jnp.float32,
    )
    return (new_top, total, summed)


def on_device(
    latent,
    fresh,
    levels,
    windows,
    plan,
    mod_table,
    w_query,
    w_key,
    w_value,
    w_out,
    query_gain,
    key_gain,
):
    queue_count = lax.axis_size("queue")
    head_count = lax.axis_size("head")
    slot = lax.axis_index("queue")
    rows = latent.shape[0]
    span = rows * head_count
    features = w_query.shape[1]
    heads_local = features // HD
    fits = latent.shape[1] % COLS == 0 and COLS == 2 * TILE
    if queue_count == heads_local and head_count == 4 and span == HD and rows % 32 == 0 and fits:
        return fused(
            latent,
            fresh,
            levels,
            windows,
            plan,
            mod_table,
            w_query,
            w_key,
            w_value,
            w_out,
            query_gain[None],
            key_gain[None],
            queue_count,
            head_count,
        )
    table_hits = levels[:, None] == jnp.arange(plan.shape[0], dtype=jnp.int32)[None, :]
    t_all = jnp.sum(jnp.where(table_hits, plan[None, :], 0), axis=1).astype(jnp.float32)
    t_from = t_all[slot]
    t_to = jnp.where(slot > 0, t_all[jnp.maximum(slot - 1, 0)], 0.0)
    step_size = (t_to - t_from) / 1000.0
    lower = jnp.maximum(0, slot - windows[slot] + 1)
    emb = embed(t_from[None], latent.shape[1])[0]
    shift = mod_table[0] + emb
    scale = mod_table[1] + emb
    gate = mod_table[2] + emb
    state = latent
    speeds = []
    new = latent
    for step in range(STEPS):
        x = state.astype(jnp.float32)
        mean = jnp.mean(x, axis=-1, keepdims=True)
        var = jnp.mean((x - mean) ** 2, axis=-1, keepdims=True)
        normed = ((x - mean) * lax.rsqrt(var + 1e-06) * (1.0 + scale) + shift).astype(jnp.bfloat16)
        piece = lax.all_gather(normed, "head", axis=0, tiled=True)
        projected = jnp.concatenate(
            [
                jnp.dot(piece, w_query, preferred_element_type=jnp.float32),
                jnp.dot(piece, w_key, preferred_element_type=jnp.float32),
                jnp.dot(piece, w_value, preferred_element_type=jnp.float32),
            ],
            axis=-1,
        )
        q = projected[:, :features]
        k = projected[:, features : 2 * features]
        values = projected[:, 2 * features :].astype(jnp.bfloat16)
        query_sq, key_sq = lax.psum((jnp.sum(q * q, axis=-1), jnp.sum(k * k, axis=-1)), "head")
        every = features * head_count
        queries = (q * lax.rsqrt(query_sq / every + 1e-06)[:, None] * query_gain).astype(
            jnp.bfloat16
        )
        keys = (k * lax.rsqrt(key_sq / every + 1e-06)[:, None] * key_gain).astype(jnp.bfloat16)
        query_heads = queries.reshape(span, heads_local, HD)
        start_carry = (
            jnp.full((heads_local, span), -1e30, jnp.float32),
            jnp.zeros((heads_local, span), jnp.float32),
            jnp.zeros((heads_local, span, HD), jnp.float32),
        )
        inner = start_carry
        piece_keys = lax.all_gather(keys, "queue", axis=0, tiled=True)
        piece_values = lax.all_gather(values, "queue", axis=0, tiled=True)
        count = piece_keys.shape[0]
        blocks = count // span

        def one_block(running, block):
            block_keys, block_values, block_index = block
            return (
                absorb(
                    running,
                    block_keys,
                    block_values,
                    block_index * span,
                    query_heads,
                    lower,
                    slot,
                    span,
                ),
                None,
            )

        inner, unused = lax.scan(
            one_block,
            inner,
            (
                piece_keys.reshape(blocks, span, features),
                piece_values.reshape(blocks, span, features),
                jnp.arange(blocks, dtype=jnp.int32),
            ),
        )
        top, total, summed = inner
        attn = (
            jnp.transpose(summed / total[:, :, None], (1, 0, 2))
            .reshape(span, features)
            .astype(jnp.bfloat16)
        )
        mixed = lax.psum_scatter(
            jnp.dot(attn, w_out, preferred_element_type=jnp.float32).astype(jnp.bfloat16),
            "head",
            scatter_dimension=0,
            tiled=True,
        ).astype(jnp.float32)
        speed = (x + gate * mixed).astype(jnp.bfloat16)
        speeds.append(speed)
        new = (x + step_size * speed.astype(jnp.float32)).astype(jnp.bfloat16)
        if step < STEPS - 1:
            moved = shifted(new, "queue", -1)
            state = jnp.where(slot == queue_count - 1, fresh, moved)
    return (jnp.stack(speeds), new)


def solution(mesh):
    return jax.shard_map(
        on_device,
        mesh=mesh,
        in_specs=(
            P(("queue", "head"), None),
            P("head", None),
            P(),
            P(),
            P(),
            P(),
            P(None, "head"),
            P(None, "head"),
            P(None, "head"),
            P("head", None),
            P("head"),
            P("head"),
        ),
        out_specs=(P(None, ("queue", "head"), None), P(("queue", "head"), None)),
        check_vma=False,
    )
```
